32 devices in a mesh: term: 2 (over y), pass: 16 (over z, x, core).
Axes of the slice: x: 2, y: 2, z: 4, core: 2. Of those that a mesh axis runs over, the one named last changes fastest.
Arguments:
- hidden: bfloat16 [8192, 4096], P('pass', 'term'), may hold values from -16 to 16
- head_weight: bfloat16 [4096, 16384], P('pass', 'term'), may hold values from -0.09375 to 0.09375
- lengths: int32 [128], P('pass'), may hold values from 1 to 64, as said below
Outputs:
- postings: bfloat16 [16384, 128], P(('term', 'pass'))
The draws below stay inside these ranges and needn't reach their ends.
Inputs may be any that keep to these rules, and one draw needn't show every extreme that they name: Passage p's valid tokens are its first lengths[p] slots; some passage has exactly 64.
All inputs are finite; a program needn't handle non-finite values.
Results may differ from the reference program's by a relative error of at most 0.013.
Values may be sent and summed in bfloat16 or wider, within the bound.
A program may use at most 128 MiB of HBM per device.

```python
import jax
import jax.numpy as jnp
from jax import lax

D = 4096
VW = 16384
LEN = 64
PASSAGES = 128
TOKENS = 8192


def draw_hidden(key, part):
    first, second = jax.random.split(key, 2)
    owners = jnp.arange(TOKENS, dtype=jnp.int32) // LEN
    rising = jnp.float32(3.0) ** (owners.astype(jnp.float32) / jnp.float32(max(PASSAGES - 1, 1)))
    values = jax.random.normal(first, (TOKENS, D), jnp.float32)
    jitter = jnp.exp(jax.random.uniform(second, (TOKENS, 1), jnp.float32, -0.55, 0.55))
    result = values * jitter * 0.8 * rising[:, None]
    return jnp.clip(result, -16.0, 16.0).astype(jnp.bfloat16)


def draw_lengths(key, part):
    first, second, third = jax.random.split(key, 3)
    counts = jax.random.randint(first, (PASSAGES,), 1, LEN + 1, dtype=jnp.int32)
    longest = jax.random.randint(second, (), 0, PASSAGES, dtype=jnp.int32)
    shortest = (longest + jax.random.randint(third, (), 1, PASSAGES, dtype=jnp.int32)) % PASSAGES
    places = jnp.arange(PASSAGES, dtype=jnp.int32)
    counts = jnp.where(places == longest, LEN, jnp.where(places == shortest, 1, counts))
    return counts.astype(jnp.int32)


def block_levels(own_key, dims, shards, smallest, high):
    factor_of = 1.0
    for position, blocks in shards:
        steps = jax.random.uniform(jax.random.fold_in(jax.random.fold_in(own_key, 6), position), (blocks,), jnp.float32, smallest / len(shards), high / len(shards))
        factor_of = factor_of * jnp.repeat(jnp.exp(steps), dims[position] // blocks).reshape((-1,) + (1,) * (len(dims) - 1 - position))
    return factor_of


def noise(key, extent, width, reach, cuts=(), held_as=jnp.bfloat16):
    level = block_levels(key, extent, cuts, -0.22, 0.18) if cuts else 1.0
    drawn = jax.random.normal(key, extent, jnp.float32) * width * level
    return jnp.minimum(jnp.maximum(drawn, -reach), reach).astype(held_as)


def setup_inputs(seed: int = 0) -> dict:
    keys = jax.random.split(jax.random.key(seed), 4)
    return {
        "hidden": draw_hidden(jax.random.fold_in(keys[3], 71), 0),
        "head_weight": noise(keys[1], (D, VW), D ** -0.5, 0.09375, ((0, 16), (1, 2))),
        "lengths": draw_lengths(jax.random.fold_in(keys[3], 71), 0),
    }


def reference(hidden, head_weight, lengths):
    block_cols = min(VW, 1024)
    positions = jnp.arange(LEN, dtype=jnp.int32)
    allowed = positions[None, :] < lengths[:, None]
    weight_blocks = head_weight.reshape(D, VW // block_cols, block_cols).transpose(1, 0, 2)

    def pooling(weight_block):
        logits = jnp.dot(hidden, weight_block, preferred_element_type=jnp.float32)
        impacts = jnp.log1p(jnp.maximum(logits, jnp.float32(0.0))).reshape(PASSAGES, LEN, block_cols)
        impacts = jnp.where(allowed[:, :, None], impacts, jnp.float32(0.0))
        return jnp.max(impacts, axis=1).astype(jnp.bfloat16)

    pooled = lax.map(pooling, weight_blocks)
    pooled = pooled.transpose(1, 0, 2).reshape(PASSAGES, VW)
    pooled_f = pooled.astype(jnp.float32)
    column_max = jnp.max(pooled_f, axis=0)
    scaled = pooled_f / (1.0 + column_max)[None, :]
    return scaled.T.astype(jnp.bfloat16)
```

```python
import jax
import jax.numpy as jnp
from jax import lax
from jax.sharding import PartitionSpec as P


def body(hidden, head_weight, lengths):
    terms = lax.axis_size("term")
    owners = lax.axis_size("pass")
    passages = lengths.shape[0]
    tokens_per = hidden.shape[0] // passages
    slab_cols = head_weight.shape[1]
    range_cols = slab_cols // owners
    own = lax.all_to_all(hidden, "term", split_axis=0, concat_axis=1, tiled=True)
    tokens = lax.all_gather(own, "pass", axis=0, tiled=True)
    rows = lax.all_to_all(head_weight, "pass", split_axis=1, concat_axis=0, tiled=True)
    weights = lax.all_gather(rows, "term", axis=1, tiled=True)
    share = passages // terms
    every = lax.all_gather(lengths, "pass", axis=0, tiled=True).reshape(owners, terms, share)
    mine = lax.dynamic_index_in_dim(every, lax.axis_index("term"), 1, False).reshape(-1)
    logits = jnp.dot(tokens, weights, preferred_element_type=jnp.float32)
    logits = logits.reshape(owners * share, tokens_per, terms * range_cols)
    allowed = jnp.arange(tokens_per, dtype=jnp.int32)[None, :] < mine[:, None]
    top = jnp.max(jnp.where(allowed[:, :, None], logits, jnp.float32(0.0)), axis=1)
    pooled = jnp.log1p(jnp.maximum(top, jnp.float32(0.0))).astype(jnp.bfloat16)
    got = lax.all_to_all(
        pooled.reshape(owners * share, terms, range_cols), "term", split_axis=1, concat_axis=1, tiled=True
    )
    full = got.reshape(owners, share, terms, range_cols).transpose(0, 2, 1, 3)
    full = full.reshape(owners * passages, range_cols).astype(jnp.float32)
    peak = jnp.max(full, axis=0)
    return jnp.transpose((full / (1.0 + peak)[None, :]).astype(jnp.bfloat16))


def solution(mesh):
    return jax.shard_map(
        body,
        mesh=mesh,
        in_specs=(P("pass", "term"), P("pass", "term"), P("pass")),
        out_specs=P(("term", "pass"), None),
        check_vma=False,
    )
```

```python
import functools

import jax
import jax.numpy as jnp
from jax import lax
from jax.experimental import pallas as pl
from jax.experimental.pallas import tpu as pltpu
from jax.sharding import PartitionSpec as P

MESH = pl.DeviceIdType.MESH
ZS, XS, CS = 4, 2, 2
CHUNKS = 4
HIGHEST_VMEM = 58 * 1024 * 1024


def kernel(
    tokens_per, hid, head, out,
    tok, wts, pool, give, take,
    s_up, s_dn, r_z, s_y, r_y, s_c, r_c, s_h, r_h, s_x, r_x, s_f, r_f, s_l,
):
    y = lax.axis_index("term")
    me = lax.axis_index("pass")
    z, x, c = me // (XS * CS), (me // CS) % XS, me % CS
    block, feats = hid.shape
    feat_rows = head.shape[0]
    cols = wts.shape[2]
    rows = block // CHUNKS
    per = block // tokens_per

    def at(zz, xx, cc):
        return (zz * XS + xx) * CS + cc

    y_dev = (1 - y, me)
    x_dev = (y, at(z, 1 - x, c))
    c_dev = (y, at(z, x, 1 - c))
    up_dev = (y, at(jnp.minimum(z + 1, ZS - 1), x, c))
    dn_dev = (y, at(jnp.maximum(z - 1, 0), x, c))

    def others(do):
        for i in range(1, ZS):
            zz = lax.rem(z + i, ZS)
            for cc in range(CS):
                do(zz, cc)
        do(z, 1 - c)

    barrier = pltpu.get_barrier_semaphore()

    def hello(dev):
        pl.semaphore_signal(barrier, inc=1, device_id=dev, device_id_type=MESH)

    others(lambda zz, cc: hello((y, at(zz, x, cc))))
    hello(x_dev)
    hello(y_dev)
    pl.semaphore_wait(barrier, ZS * CS + 1)

    def remote(src, dst, send, recv, dev):
        return pltpu.make_async_remote_copy(
            src_ref=src, dst_ref=dst, send_sem=send, recv_sem=recv,
            device_id=dev, device_id_type=MESH,
        )

    def piece(f, zz, cc, k):
        return tok.at[f, zz, cc, pl.ds(k * rows, rows)]

    def own_piece(k):
        return hid.at[pl.ds(k * rows, rows)]

    def up(zz, k, src):
        return remote(src, piece(y, zz, c, k), s_up.at[zz, k], r_z.at[zz, k], up_dev)

    def down(zz, k, src):
        return remote(src, piece(y, zz, c, k), s_dn.at[zz, k], r_z.at[zz, k], dn_dev)

    def across_y(zz, k, src):
        return remote(src, piece(y, zz, c, k), s_y.at[zz, k], r_y.at[zz, k], y_dev)

    def across_c(f, zz, k, src):
        return remote(src, piece(f, zz, c, k), s_c.at[f, zz, k], r_c.at[f, zz, k], c_dev)

    def strip(zz, cc, xx):
        first = at(zz, xx, cc) * cols
        return head.at[:, pl.ds(pl.multiple_of(first, cols), cols)]

    def wts_of(p, xx):
        return wts.at[xx, pl.ds(pl.multiple_of(p * feat_rows, feat_rows), feat_rows)]

    def both_of(p):
        return wts.at[:, pl.ds(pl.multiple_of(p * feat_rows, feat_rows), feat_rows)]

    def head_to(zz, cc, xx):
        return remote(
            strip(zz, cc, xx), wts_of(me, xx),
            s_h.at[zz * CS + cc, xx], r_h.at[z * CS + c, xx], (y, at(zz, x, cc)),
        )

    def head_from(zz, cc, xx):
        ref = wts_of(at(zz, x, cc), xx)
        return remote(ref, ref, s_h.at[zz * CS + cc, xx], r_h.at[zz * CS + cc, xx], x_dev)

    def relay(zz, cc):
        ref = both_of(at(zz, x, cc))
        return remote(ref, ref, s_x.at[zz * CS + cc], r_x.at[zz * CS + cc], x_dev)

    def send_head(zz, cc):
        for xx in range(XS):
            head_to(zz, cc, xx).start()

    others(send_head)
    local = [pltpu.make_async_copy(strip(z, c, xx), wts_of(me, xx), s_l.at[xx]) for xx in range(XS)]
    local.append(pltpu.make_async_copy(hid, tok.at[y, z, c], s_l.at[XS]))
    for copy in local:
        copy.start()
    for k in range(CHUNKS):
        @pl.when(z < ZS - 1)
        def _():
            up(z, k, own_piece(k)).start()

        @pl.when(z > 0)
        def _():
            down(z, k, own_piece(k)).start()

        across_y(z, k, own_piece(k)).start()
        across_c(y, z, k, own_piece(k)).start()
    for copy in local:
        copy.wait()
    relay(z, c).start()

    def pass_head(zz, cc):
        for xx in range(XS):
            head_from(zz, cc, xx).wait_recv()
        relay(zz, cc).start()

    others(pass_head)

    def multiply(zz, cc):
        def half(xx, carry):
            acc = jnp.dot(tok[0, zz, cc], wts[xx, pl.ds(0, feats)], preferred_element_type=jnp.float32)
            acc += jnp.dot(tok[1, zz, cc], wts[xx, pl.ds(feats, feats)], preferred_element_type=jnp.float32)
            top = jnp.max(acc.reshape(per, tokens_per, cols), axis=1)
            first = pl.multiple_of((zz * CS + cc) * per, per)
            pool[xx, pl.ds(first, per), :] = jnp.log1p(jnp.maximum(top, 0.0))
            return carry

        lax.fori_loop(0, XS, half, 0)

    def step(d, carry):
        for k in range(CHUNKS):
            below, above = z - d - 1, z + d + 1

            @pl.when(below >= 0)
            def _():
                src = piece(y, below, c, k)
                up(below, k, src).wait_recv()

                @pl.when(z < ZS - 1)
                def _():
                    up(below, k, src).start()

                across_y(below, k, src).start()
                across_c(y, below, k, src).start()

            @pl.when(above < ZS)
            def _():
                src = piece(y, above, c, k)
                down(above, k, src).wait_recv()

                @pl.when(z > 0)
                def _():
                    down(above, k, src).start()

                across_y(above, k, src).start()
                across_c(y, above, k, src).start()

        def sides(do):
            def side(s, inner):
                zz = z + (1 - 2 * s) * d

                @pl.when((zz >= 0) & (zz < ZS) & ((d > 0) | (s == 0)))
                def _():
                    do(zz)

                return inner

            lax.fori_loop(0, 2, side, 0)

        def from_y(zz):
            for k in range(CHUNKS):
                src = piece(1 - y, zz, c, k)
                across_y(zz, k, src).wait_recv()
                across_c(1 - y, zz, k, src).start()

        sides(from_y)

        @pl.when(d == 0)
        def _():
            for i in range(ZS * CS):
                relay(i // CS, i % CS).wait_recv()

        def use(zz):
            def core(i, inner):
                cc = lax.rem(c + i, CS)

                @pl.when(i == 1)
                def _():
                    for f in range(2):
                        for k in range(CHUNKS):
                            across_c(f, zz, k, piece(f, zz, c, k)).wait_recv()

                multiply(zz, cc)
                return inner

            lax.fori_loop(0, CS, core, 0)

        sides(use)
        return carry

    lax.fori_loop(0, ZS, step, 0)

    give[...] = pool[1 - x].astype(jnp.bfloat16)
    last = remote(give, take, s_f, r_f, x_dev)
    last.start()

    def sent(zz, carry):
        for k in range(CHUNKS):
            @pl.when((zz <= z) & (z < ZS - 1))
            def _():
                up(zz, k, own_piece(k)).wait_send()

            @pl.when((zz >= z) & (z > 0))
            def _():
                down(zz, k, own_piece(k)).wait_send()

            across_y(zz, k, own_piece(k)).wait_send()
            for f in range(2):
                across_c(f, zz, k, own_piece(k)).wait_send()
        for cc in range(CS):
            relay(zz, cc).wait_send()
        return carry

    lax.fori_loop(0, ZS, sent, 0)

    def head_sent(zz, cc):
        for xx in range(XS):
            head_to(zz, cc, xx).wait_send()

    others(head_sent)
    last.wait()

    mine = pool[x].astype(jnp.bfloat16).astype(jnp.float32)
    theirs = take[...].astype(jnp.float32)
    even = jnp.where(x == 0, mine, theirs)
    odd = jnp.where(x == 0, theirs, mine)
    span = CS * per
    parts = []
    for zz in range(ZS):
        parts += [even[zz * span:(zz + 1) * span], odd[zz * span:(zz + 1) * span]]
    full = jnp.concatenate(parts, axis=0)
    peak = jnp.max(full, axis=0, keepdims=True)
    out[...] = jnp.transpose(full / (1.0 + peak)).astype(jnp.bfloat16)


def masked(hidden, lengths):
    passages = lengths.shape[0]
    tokens_per = hidden.shape[0] // passages
    allowed = jnp.arange(tokens_per, dtype=jnp.int32)[None, :] < lengths[:, None]
    return jnp.where(allowed.reshape(-1)[:, None], hidden, jnp.bfloat16(0.0))


def fused(hidden, head_weight, lengths):
    passages = lengths.shape[0]
    tokens = hidden.shape[0]
    feats = hidden.shape[1]
    feat_rows = head_weight.shape[0]
    cols = head_weight.shape[1] // (ZS * XS * CS)
    rows = ZS * CS * passages
    dma = pltpu.SemaphoreType.DMA
    return pl.pallas_call(
        functools.partial(kernel, tokens // passages),
        out_shape=jax.ShapeDtypeStruct((cols, XS * rows), jnp.bfloat16),
        in_specs=[pl.BlockSpec(memory_space=pl.ANY)] * 2,
        out_specs=pl.BlockSpec(memory_space=pltpu.VMEM),
        scratch_shapes=[
            pltpu.VMEM((2, ZS, CS, tokens, feats), jnp.bfloat16),
            pltpu.VMEM((XS, 2 * feats, cols), jnp.bfloat16),
            pltpu.VMEM((XS, rows, cols), jnp.float32),
            pltpu.VMEM((rows, cols), jnp.bfloat16),
            pltpu.VMEM((rows, cols), jnp.bfloat16),
            dma((ZS, CHUNKS)), dma((ZS, CHUNKS)), dma((ZS, CHUNKS)),
            dma((ZS, CHUNKS)), dma((ZS, CHUNKS)),
            dma((2, ZS, CHUNKS)), dma((2, ZS, CHUNKS)),
            dma((ZS * CS, XS)), dma((ZS * CS, XS)),
            dma((ZS * CS,)), dma((ZS * CS,)),
            dma, dma, dma((XS + 1,)),
        ],
        compiler_params=pltpu.CompilerParams(
            collective_id=0, has_side_effects=True, vmem_limit_bytes=HIGHEST_VMEM
        ),
        cost_estimate=pl.CostEstimate(
            flops=2 * ZS * CS * tokens * 2 * feats * XS * cols,
            bytes_accessed=2 * (tokens * feats + feat_rows * head_weight.shape[1]),
            transcendentals=0,
        ),
    )(masked(hidden, lengths), head_weight)


def general(hidden, head_weight, lengths):
    terms = lax.axis_size("term")
    owners = lax.axis_size("pass")
    passages = lengths.shape[0]
    tokens_per = hidden.shape[0] // passages
    range_cols = head_weight.shape[1] // owners
    own = lax.all_to_all(masked(hidden, lengths), "term", split_axis=0, concat_axis=1, tiled=True)
    tokens = lax.all_gather(own, "pass", axis=0, tiled=True)
    rows = lax.all_to_all(head_weight, "pass", split_axis=1, concat_axis=0, tiled=True)
    weights = lax.all_gather(rows, "term", axis=1, tiled=True)
    share = passages // terms
    logits = jnp.dot(tokens, weights, preferred_element_type=jnp.float32)
    logits = logits.reshape(owners * share, tokens_per, terms * range_cols)
    top = jnp.maximum(jnp.max(logits, axis=1), jnp.float32(0.0))
    pooled = jnp.log1p(top).astype(jnp.bfloat16)
    got = lax.all_to_all(
        pooled.reshape(owners * share, terms, range_cols), "term", split_axis=1, concat_axis=1, tiled=True
    )
    full = got.reshape(owners, share, terms, range_cols).transpose(0, 2, 1, 3)
    full = full.reshape(owners * passages, range_cols).astype(jnp.float32)
    peak = jnp.max(full, axis=0)
    return jnp.transpose((full / (1.0 + peak)[None, :]).astype(jnp.bfloat16))


def solution(mesh):
    small = mesh.shape["term"] == 2 and mesh.shape["pass"] == ZS * XS * CS
    return jax.shard_map(
        fused if small else general,
        mesh=mesh,
        in_specs=(P("pass", "term"), P("pass", "term"), P("pass")),
        out_specs=P(("term", "pass"), None),
        check_vma=False,
    )
```

```python
import functools

import jax
import jax.numpy as jnp
from jax import lax
from jax.experimental import pallas as pl
from jax.experimental.pallas import tpu as pltpu
from jax.sharding import PartitionSpec as P

MESH = pl.DeviceIdType.MESH
ZS, XS, CS = 4, 2, 2
CHUNKS = 4
STEPS = 4
HIGHEST_VMEM = 58 * 1024 * 1024


def kernel(
    tokens_per, hid, head, out,
    tok, wts, pool, give, take,
    s_up, s_dn, r_z, s_y, r_y, s_c, r_c, s_h, r_h, s_x, r_x, s_f, r_f, s_l,
):
    y = lax.axis_index("term")
    me = lax.axis_index("pass")
    z, x, c = me // (XS * CS), (me // CS) % XS, me % CS
    block, feats = hid.shape
    feat_rows = head.shape[0]
    cols = wts.shape[2]
    rows = block // CHUNKS
    per = block // tokens_per

    def at(zz, xx, cc):
        return (zz * XS + xx) * CS + cc

    y_dev = (1 - y, me)
    x_dev = (y, at(z, 1 - x, c))
    c_dev = (y, at(z, x, 1 - c))
    up_dev = (y, at(jnp.minimum(z + 1, ZS - 1), x, c))
    dn_dev = (y, at(jnp.maximum(z - 1, 0), x, c))

    def others(do):
        for i in range(1, ZS):
            zz = lax.rem(z + i, ZS)
            for cc in range(CS):
                do(zz, cc)
        do(z, 1 - c)

    barrier = pltpu.get_barrier_semaphore()

    def hello(dev):
        pl.semaphore_signal(barrier, inc=1, device_id=dev, device_id_type=MESH)

    others(lambda zz, cc: hello((y, at(zz, x, cc))))
    hello(x_dev)
    hello(y_dev)
    pl.semaphore_wait(barrier, ZS * CS + 1)

    def remote(src, dst, send, recv, dev):
        return pltpu.make_async_remote_copy(
            src_ref=src, dst_ref=dst, send_sem=send, recv_sem=recv,
            device_id=dev, device_id_type=MESH,
        )

    def piece(f, zz, cc, k):
        return tok.at[f, zz, cc, pl.ds(k * rows, rows)]

    def own_piece(k):
        return hid.at[pl.ds(k * rows, rows)]

    def up(zz, k, src):
        return remote(src, piece(y, zz, c, k), s_up.at[zz, k], r_z.at[zz, k], up_dev)

    def down(zz, k, src):
        return remote(src, piece(y, zz, c, k), s_dn.at[zz, k], r_z.at[zz, k], dn_dev)

    def across_y(zz, k, src):
        return remote(src, piece(y, zz, c, k), s_y.at[zz, k], r_y.at[zz, k], y_dev)

    def across_c(f, zz, k, src):
        return remote(src, piece(f, zz, c, k), s_c.at[f, zz, k], r_c.at[f, zz, k], c_dev)

    def strip(zz, cc, xx):
        first = at(zz, xx, cc) * cols
        return head.at[:, pl.ds(pl.multiple_of(first, cols), cols)]

    def wts_of(p, xx):
        return wts.at[xx, pl.ds(pl.multiple_of(p * feat_rows, feat_rows), feat_rows)]

    def head_to(zz, cc, xx):
        return remote(
            strip(zz, cc, xx), wts_of(me, xx),
            s_h.at[zz * CS + cc, xx], r_h.at[z * CS + c, xx], (y, at(zz, x, cc)),
        )

    def head_from(zz, cc, xx):
        ref = wts_of(at(zz, x, cc), xx)
        return remote(ref, ref, s_h.at[zz * CS + cc, xx], r_h.at[zz * CS + cc, xx], x_dev)

    def relay(zz, cc, xx):
        ref = wts_of(at(zz, x, cc), xx)
        return remote(ref, ref, s_x.at[zz * CS + cc, xx], r_x.at[zz * CS + cc, xx], x_dev)

    def relay_from(zz, cc, xx):
        ref = wts_of(at(zz, 1 - x, cc), xx)
        return remote(ref, ref, s_x.at[zz * CS + cc, xx], r_x.at[zz * CS + cc, xx], x_dev)

    def send_head(xx):
        others(lambda zz, cc: head_to(zz, cc, xx).start())
        relay(z, c, xx).start()

    def pass_head(zz, cc, xx):
        head_from(zz, cc, xx).wait_recv()
        relay(zz, cc, xx).start()

    def sides(d, do):
        def side(s, inner):
            zz = z + (1 - 2 * s) * d

            @pl.when((zz >= 0) & (zz < ZS))
            def _():
                do(zz)

            return inner

        lax.fori_loop(0, 2, side, 0)

    def pass_tokens(d, k):
        below, above = z - d, z + d

        @pl.when(below >= 0)
        def _():
            src = piece(y, below, c, k)
            up(below, k, src).wait_recv()

            @pl.when(z < ZS - 1)
            def _():
                up(below, k, src).start()

            across_y(below, k, src).start()
            across_c(y, below, k, src).start()

        @pl.when(above < ZS)
        def _():
            src = piece(y, above, c, k)
            down(above, k, src).wait_recv()

            @pl.when(z > 0)
            def _():
                down(above, k, src).start()

            across_y(above, k, src).start()
            across_c(y, above, k, src).start()

    def from_y(zz):
        def one(k, carry):
            src = piece(1 - y, zz, c, k)
            across_y(zz, k, src).wait_recv()
            across_c(1 - y, zz, k, src).start()
            return carry

        lax.fori_loop(0, CHUNKS, one, 0)

    def pass_far_head(d):
        def both(zz):
            for cc in range(CS):
                pass_head(zz, cc, 1)

        sides(d, both)

    def send_own(k, carry):
        @pl.when(z < ZS - 1)
        def _():
            up(z, k, own_piece(k)).start()

        @pl.when(z > 0)
        def _():
            down(z, k, own_piece(k)).start()

        across_y(z, k, own_piece(k)).start()
        across_c(y, z, k, own_piece(k)).start()
        return carry

    lax.fori_loop(0, CHUNKS, send_own, 0)
    local = [pltpu.make_async_copy(strip(z, c, xx), wts_of(me, xx), s_l.at[xx]) for xx in range(XS)]
    local.append(pltpu.make_async_copy(hid, tok.at[y, z, c], s_l.at[XS]))
    for copy in local:
        copy.start()
    for copy in local:
        copy.wait()

    def first(k, carry):
        @pl.when(k == CHUNKS // 2)
        def _():
            send_head(0)

        pass_tokens(1, k)
        return carry

    def second(k, carry):
        pass_tokens(2, k)
        return carry

    lax.fori_loop(0, CHUNKS, first, 0)
    from_y(z)
    lax.fori_loop(0, CHUNKS, second, 0)
    send_head(1)
    others(lambda zz, cc: pass_head(zz, cc, 0))
    pass_head(z, 1 - c, 1)
    sides(1, from_y)

    def arrived(zz):
        for f in range(2):
            for k in range(CHUNKS):
                across_c(f, zz, k, piece(f, zz, 1 - c, k)).wait_recv()

    def multiply(zz, cc, xx):
        acc = jnp.dot(tok[0, zz, cc], wts[xx, pl.ds(0, feats)], preferred_element_type=jnp.float32)
        acc += jnp.dot(tok[1, zz, cc], wts[xx, pl.ds(feats, feats)], preferred_element_type=jnp.float32)
        top = jnp.max(acc.reshape(per, tokens_per, cols), axis=1)
        start = pl.multiple_of((zz * CS + cc) * per, per)
        pool[xx, pl.ds(start, per), :] = jnp.log1p(jnp.maximum(top, 0.0))

    def step(j, carry):
        @pl.when(j < STEPS)
        def _():
            for i in range(CHUNKS // STEPS):
                pass_tokens(3, j * (CHUNKS // STEPS) + i)

        @pl.when(j == 0)
        def _():
            for i in range(ZS * CS):
                relay_from(i // CS, i % CS, 0).wait_recv()

        @pl.when(j == STEPS - 1)
        def _():
            pass_far_head(1)
            sides(2, from_y)

        @pl.when(j == STEPS + 1)
        def _():
            pass_far_head(2)
            sides(3, from_y)
            pass_far_head(3)

        d, s = (j + 1) // 2, (j + 1) % 2
        zz = z + (1 - 2 * s) * d

        @pl.when((zz >= 0) & (zz < ZS))
        def _():
            arrived(zz)

            def core(cc, inner):
                multiply(zz, cc, 0)
                return inner

            lax.fori_loop(0, CS, core, 0)

        return carry

    lax.fori_loop(0, 2 * ZS - 1, step, 0)
    for i in range(ZS * CS):
        relay_from(i // CS, i % CS, 1).wait_recv()

    def rest(i, carry):
        multiply(i // CS, i % CS, 1)
        return carry

    lax.fori_loop(0, ZS * CS, rest, 0)

    give[...] = pool[1 - x].astype(jnp.bfloat16)
    last = remote(give, take, s_f, r_f, x_dev)
    last.start()

    def sent(zz, carry):
        for k in range(CHUNKS):
            @pl.when((zz <= z) & (z < ZS - 1))
            def _():
                up(zz, k, own_piece(k)).wait_send()

            @pl.when((zz >= z) & (z > 0))
            def _():
                down(zz, k, own_piece(k)).wait_send()

            across_y(zz, k, own_piece(k)).wait_send()
            for f in range(2):
                across_c(f, zz, k, own_piece(k)).wait_send()
        for cc in range(CS):
            for xx in range(XS):
                relay(zz, cc, xx).wait_send()
        return carry

    lax.fori_loop(0, ZS, sent, 0)

    def head_sent(zz, cc):
        for xx in range(XS):
            head_to(zz, cc, xx).wait_send()

    others(head_sent)
    last.wait()

    mine = pool[x].astype(jnp.bfloat16).astype(jnp.float32)
    theirs = take[...].astype(jnp.float32)
    even = jnp.where(x == 0, mine, theirs)
    odd = jnp.where(x == 0, theirs, mine)
    span = CS * per
    parts = []
    for zz in range(ZS):
        parts += [even[zz * span:(zz + 1) * span], odd[zz * span:(zz + 1) * span]]
    full = jnp.concatenate(parts, axis=0)
    peak = jnp.max(full, axis=0, keepdims=True)
    out[...] = jnp.transpose(full / (1.0 + peak)).astype(jnp.bfloat16)


def masked(hidden, lengths):
    passages = lengths.shape[0]
    tokens_per = hidden.shape[0] // passages
    allowed = jnp.arange(tokens_per, dtype=jnp.int32)[None, :] < lengths[:, None]
    return jnp.where(allowed.reshape(-1)[:, None], hidden, jnp.bfloat16(0.0))


def fused(hidden, head_weight, lengths):
    passages = lengths.shape[0]
    tokens = hidden.shape[0]
    feats = hidden.shape[1]
    feat_rows = head_weight.shape[0]
    cols = head_weight.shape[1] // (ZS * XS * CS)
    rows = ZS * CS * passages
    dma = pltpu.SemaphoreType.DMA
    return pl.pallas_call(
        functools.partial(kernel, tokens // passages),
        out_shape=jax.ShapeDtypeStruct((cols, XS * rows), jnp.bfloat16),
        in_specs=[pl.BlockSpec(memory_space=pl.ANY)] * 2,
        out_specs=pl.BlockSpec(memory_space=pltpu.VMEM),
        scratch_shapes=[
            pltpu.VMEM((2, ZS, CS, tokens, feats), jnp.bfloat16),
            pltpu.VMEM((XS, 2 * feats, cols), jnp.bfloat16),
            pltpu.VMEM((XS, rows, cols), jnp.float32),
            pltpu.VMEM((rows, cols), jnp.bfloat16),
            pltpu.VMEM((rows, cols), jnp.bfloat16),
            dma((ZS, CHUNKS)), dma((ZS, CHUNKS)), dma((ZS, CHUNKS)),
            dma((ZS, CHUNKS)), dma((ZS, CHUNKS)),
            dma((2, ZS, CHUNKS)), dma((2, ZS, CHUNKS)),
            dma((ZS * CS, XS)), dma((ZS * CS, XS)),
            dma((ZS * CS, XS)), dma((ZS * CS, XS)),
            dma, dma, dma((XS + 1,)),
        ],
        compiler_params=pltpu.CompilerParams(
            collective_id=0, has_side_effects=True, vmem_limit_bytes=HIGHEST_VMEM
        ),
        cost_estimate=pl.CostEstimate(
            flops=2 * ZS * CS * tokens * 2 * feats * XS * cols,
            bytes_accessed=2 * (tokens * feats + feat_rows * head_weight.shape[1]),
            transcendentals=0,
        ),
    )(masked(hidden, lengths), head_weight)


def general(hidden, head_weight, lengths):
    terms = lax.axis_size("term")
    owners = lax.axis_size("pass")
    passages = lengths.shape[0]
    tokens_per = hidden.shape[0] // passages
    range_cols = head_weight.shape[1] // owners
    own = lax.all_to_all(masked(hidden, lengths), "term", split_axis=0, concat_axis=1, tiled=True)
    tokens = lax.all_gather(own, "pass", axis=0, tiled=True)
    rows = lax.all_to_all(head_weight, "pass", split_axis=1, concat_axis=0, tiled=True)
    weights = lax.all_gather(rows, "term", axis=1, tiled=True)
    share = passages // terms
    logits = jnp.dot(tokens, weights, preferred_element_type=jnp.float32)
    logits = logits.reshape(owners * share, tokens_per, terms * range_cols)
    top = jnp.maximum(jnp.max(logits, axis=1), jnp.float32(0.0))
    pooled = jnp.log1p(top).astype(jnp.bfloat16)
    got = lax.all_to_all(
        pooled.reshape(owners * share, terms, range_cols), "term", split_axis=1, concat_axis=1, tiled=True
    )
    full = got.reshape(owners, share, terms, range_cols).transpose(0, 2, 1, 3)
    full = full.reshape(owners * passages, range_cols).astype(jnp.float32)
    peak = jnp.max(full, axis=0)
    return jnp.transpose((full / (1.0 + peak)[None, :]).astype(jnp.bfloat16))


def solution(mesh):
    small = mesh.shape["term"] == 2 and mesh.shape["pass"] == ZS * XS * CS
    return jax.shard_map(
        fused if small else general,
        mesh=mesh,
        in_specs=(P("pass", "term"), P("pass", "term"), P("pass")),
        out_specs=P(("term", "pass"), None),
        check_vma=False,
    )
```

```python
import jax
import jax.numpy as jnp
from jax import lax
from jax.experimental import pallas as pl
from jax.experimental.pallas import tpu as pltpu
from jax.sharding import PartitionSpec as P

MESH = pl.DeviceIdType.MESH
ZS, XS, CS = 4, 2, 2
CHUNKS = 4


def kernel(
    hid, head, tok, wts,
    s_up, s_dn, r_z, s_y, r_y, s_c, r_c, s_h, r_h, s_x, r_x, s_l,
):
    y = lax.axis_index("term")
    me = lax.axis_index("pass")
    z, x, c = me // (XS * CS), (me // CS) % XS, me % CS
    block, feats = hid.shape
    feat_rows = head.shape[0]
    cols = wts.shape[1] // XS
    rows = block // CHUNKS

    def at(zz, xx, cc):
        return (zz * XS + xx) * CS + cc

    y_dev = (1 - y, me)
    x_dev = (y, at(z, 1 - x, c))
    c_dev = (y, at(z, x, 1 - c))
    up_dev = (y, at(jnp.minimum(z + 1, ZS - 1), x, c))
    dn_dev = (y, at(jnp.maximum(z - 1, 0), x, c))

    def others(do):
        for i in range(1, ZS):
            zz = lax.rem(z + i, ZS)
            for cc in range(CS):
                do(zz, cc)
        do(z, 1 - c)

    barrier = pltpu.get_barrier_semaphore()

    def hello(dev):
        pl.semaphore_signal(barrier, inc=1, device_id=dev, device_id_type=MESH)

    others(lambda zz, cc: hello((y, at(zz, x, cc))))
    hello(x_dev)
    hello(y_dev)
    pl.semaphore_wait(barrier, ZS * CS + 1)

    def remote(src, dst, send, recv, dev):
        return pltpu.make_async_remote_copy(
            src_ref=src, dst_ref=dst, send_sem=send, recv_sem=recv,
            device_id=dev, device_id_type=MESH,
        )

    def piece(f, zz, cc, k):
        first = (zz * CS + cc) * block + k * rows
        return tok.at[pl.ds(pl.multiple_of(first, rows), rows), pl.ds(pl.multiple_of(f * feats, feats), feats)]

    def own_piece(k):
        return hid.at[pl.ds(k * rows, rows)]

    def up(zz, k, src):
        return remote(src, piece(y, zz, c, k), s_up.at[zz, k], r_z.at[zz, k], up_dev)

    def down(zz, k, src):
        return remote(src, piece(y, zz, c, k), s_dn.at[zz, k], r_z.at[zz, k], dn_dev)

    def across_y(zz, k, src):
        return remote(src, piece(y, zz, c, k), s_y.at[zz, k], r_y.at[zz, k], y_dev)

    def across_c(f, zz, k, src):
        return remote(src, piece(f, zz, c, k), s_c.at[f, zz, k], r_c.at[f, zz, k], c_dev)

    def strip(zz, cc, xx):
        first = at(zz, xx, cc) * cols
        return head.at[:, pl.ds(pl.multiple_of(first, cols), cols)]

    def wts_of(p, xx):
        return wts.at[pl.ds(pl.multiple_of(p * feat_rows, feat_rows), feat_rows), pl.ds(xx * cols, cols)]

    def head_to(zz, cc, xx):
        return remote(
            strip(zz, cc, xx), wts_of(me, xx),
            s_h.at[zz * CS + cc, xx], r_h.at[z * CS + c, xx], (y, at(zz, x, cc)),
        )

    def head_from(zz, cc, xx):
        ref = wts_of(at(zz, x, cc), xx)
        return remote(ref, ref, s_h.at[zz * CS + cc, xx], r_h.at[zz * CS + cc, xx], x_dev)

    def relay(zz, cc, xx):
        ref = wts_of(at(zz, x, cc), xx)
        return remote(ref, ref, s_x.at[zz * CS + cc, xx], r_x.at[zz * CS + cc, xx], x_dev)

    def relay_from(zz, cc, xx):
        ref = wts_of(at(zz, 1 - x, cc), xx)
        return remote(ref, ref, s_x.at[zz * CS + cc, xx], r_x.at[zz * CS + cc, xx], x_dev)

    def send_head(xx):
        others(lambda zz, cc: head_to(zz, cc, xx).start())
        relay(z, c, xx).start()

    def pass_head(zz, cc, xx):
        head_from(zz, cc, xx).wait_recv()
        relay(zz, cc, xx).start()

    def sides(d, do):
        def side(s, inner):
            zz = z + (1 - 2 * s) * d

            @pl.when((zz >= 0) & (zz < ZS))
            def _():
                do(zz)

            return inner

        lax.fori_loop(0, 2, side, 0)

    def pass_tokens(d, k):
        below, above = z - d, z + d

        @pl.when(below >= 0)
        def _():
            src = piece(y, below, c, k)
            up(below, k, src).wait_recv()

            @pl.when(z < ZS - 1)
            def _():
                up(below, k, src).start()

            across_y(below, k, src).start()
            across_c(y, below, k, src).start()

        @pl.when(above < ZS)
        def _():
            src = piece(y, above, c, k)
            down(above, k, src).wait_recv()

            @pl.when(z > 0)
            def _():
                down(above, k, src).start()

            across_y(above, k, src).start()
            across_c(y, above, k, src).start()

    def from_y(zz):
        def one(k, carry):
            src = piece(1 - y, zz, c, k)
            across_y(zz, k, src).wait_recv()
            across_c(1 - y, zz, k, src).start()
            return carry

        lax.fori_loop(0, CHUNKS, one, 0)

    def send_own(k, carry):
        @pl.when(z < ZS - 1)
        def _():
            up(z, k, own_piece(k)).start()

        @pl.when(z > 0)
        def _():
            down(z, k, own_piece(k)).start()

        across_y(z, k, own_piece(k)).start()
        across_c(y, z, k, own_piece(k)).start()
        return carry

    lax.fori_loop(0, CHUNKS, send_own, 0)
    local = [pltpu.make_async_copy(strip(z, c, xx), wts_of(me, xx), s_l.at[xx]) for xx in range(XS)]
    whole = tok.at[pl.ds(pl.multiple_of((z * CS + c) * block, block), block), pl.ds(pl.multiple_of(y * feats, feats), feats)]
    local.append(pltpu.make_async_copy(hid, whole, s_l.at[XS]))
    for copy in local:
        copy.start()
    for copy in local:
        copy.wait()

    for xx in range(XS):
        send_head(xx)

    def pass_all(d, carry):
        for k in range(CHUNKS):
            pass_tokens(d, k)

        @pl.when(d == 1)
        def _():
            for xx in range(XS):
                pass_head(z, 1 - c, xx)

        def both(zz):
            for cc in range(CS):
                for xx in range(XS):
                    pass_head(zz, cc, xx)

        sides(d, both)

        @pl.when(d == 1)
        def _():
            from_y(z)

        @pl.when(d > 1)
        def _():
            sides(d - 1, from_y)

        return carry

    lax.fori_loop(1, ZS, pass_all, 0)
    sides(ZS - 1, from_y)
    for i in range(ZS * CS):
        for xx in range(XS):
            relay_from(i // CS, i % CS, xx).wait_recv()

    def arrived(zz, carry):
        for f in range(2):
            for k in range(CHUNKS):
                across_c(f, zz, k, piece(f, zz, 1 - c, k)).wait_recv()
        return carry

    lax.fori_loop(0, ZS, arrived, 0)

    def sent(zz, carry):
        for k in range(CHUNKS):
            @pl.when((zz <= z) & (z < ZS - 1))
            def _():
                up(zz, k, own_piece(k)).wait_send()

            @pl.when((zz >= z) & (z > 0))
            def _():
                down(zz, k, own_piece(k)).wait_send()

            across_y(zz, k, own_piece(k)).wait_send()
            for f in range(2):
                across_c(f, zz, k, own_piece(k)).wait_send()
        for cc in range(CS):
            for xx in range(XS):
                relay(zz, cc, xx).wait_send()
        return carry

    lax.fori_loop(0, ZS, sent, 0)

    def head_sent(zz, cc):
        for xx in range(XS):
            head_to(zz, cc, xx).wait_send()

    others(head_sent)


def masked(hidden, lengths):
    passages = lengths.shape[0]
    tokens_per = hidden.shape[0] // passages
    allowed = jnp.arange(tokens_per, dtype=jnp.int32)[None, :] < lengths[:, None]
    return jnp.where(allowed.reshape(-1)[:, None], hidden, jnp.bfloat16(0.0))


def fused(hidden, head_weight, lengths):
    passages = lengths.shape[0]
    tokens, feats = hidden.shape
    tokens_per = tokens // passages
    owners = ZS * XS * CS
    cols = head_weight.shape[1] // owners
    dma = pltpu.SemaphoreType.DMA
    gathered, weights = pl.pallas_call(
        kernel,
        out_shape=(
            jax.ShapeDtypeStruct((ZS * CS * tokens, 2 * feats), jnp.bfloat16),
            jax.ShapeDtypeStruct((2 * feats, XS * cols), jnp.bfloat16),
        ),
        in_specs=[pl.BlockSpec(memory_space=pl.ANY)] * 2,
        out_specs=[pl.BlockSpec(memory_space=pl.ANY)] * 2,
        scratch_shapes=[
            dma((ZS, CHUNKS)), dma((ZS, CHUNKS)), dma((ZS, CHUNKS)),
            dma((ZS, CHUNKS)), dma((ZS, CHUNKS)),
            dma((2, ZS, CHUNKS)), dma((2, ZS, CHUNKS)),
            dma((ZS * CS, XS)), dma((ZS * CS, XS)),
            dma((ZS * CS, XS)), dma((ZS * CS, XS)),
            dma((XS + 1,)),
        ],
        compiler_params=pltpu.CompilerParams(collective_id=0, has_side_effects=True),
    )(masked(hidden, lengths), head_weight)
    logits = jnp.dot(gathered, weights, preferred_element_type=jnp.float32)
    top = jnp.max(logits.reshape(ZS * CS * passages, tokens_per, XS * cols), axis=1)
    pooled = jnp.log1p(jnp.maximum(top, 0.0)).astype(jnp.bfloat16)
    x = (lax.axis_index("pass") // CS) % XS
    swap = [(p, p + CS if (p // CS) % XS == 0 else p - CS) for p in range(owners)]
    mine = lax.dynamic_slice_in_dim(pooled, x * cols, cols, 1)
    theirs = lax.ppermute(lax.dynamic_slice_in_dim(pooled, (1 - x) * cols, cols, 1), "pass", swap)
    even = jnp.where(x == 0, mine, theirs).reshape(ZS, CS * passages, cols)
    odd = jnp.where(x == 0, theirs, mine).reshape(ZS, CS * passages, cols)
    full = jnp.stack([even, odd], axis=1).reshape(owners * passages, cols).astype(jnp.float32)
    peak = jnp.max(full, axis=0)
    return jnp.transpose((full / (1.0 + peak)[None, :]).astype(jnp.bfloat16))


def general(hidden, head_weight, lengths):
    terms = lax.axis_size("term")
    owners = lax.axis_size("pass")
    passages = lengths.shape[0]
    tokens_per = hidden.shape[0] // passages
    range_cols = head_weight.shape[1] // owners
    own = lax.all_to_all(masked(hidden, lengths), "term", split_axis=0, concat_axis=1, tiled=True)
    tokens = lax.all_gather(own, "pass", axis=0, tiled=True)
    rows = lax.all_to_all(head_weight, "pass", split_axis=1, concat_axis=0, tiled=True)
    weights = lax.all_gather(rows, "term", axis=1, tiled=True)
    share = passages // terms
    logits = jnp.dot(tokens, weights, preferred_element_type=jnp.float32)
    logits = logits.reshape(owners * share, tokens_per, terms * range_cols)
    top = jnp.maximum(jnp.max(logits, axis=1), jnp.float32(0.0))
    pooled = jnp.log1p(top).astype(jnp.bfloat16)
    got = lax.all_to_all(
        pooled.reshape(owners * share, terms, range_cols), "term", split_axis=1, concat_axis=1, tiled=True
    )
    full = got.reshape(owners, share, terms, range_cols).transpose(0, 2, 1, 3)
    full = full.reshape(owners * passages, range_cols).astype(jnp.float32)
    peak = jnp.max(full, axis=0)
    return jnp.transpose((full / (1.0 + peak)[None, :]).astype(jnp.bfloat16))


def solution(mesh):
    small = mesh.shape["term"] == 2 and mesh.shape["pass"] == ZS * XS * CS
    return jax.shard_map(
        fused if small else general,
        mesh=mesh,
        in_specs=(P("pass", "term"), P("pass", "term"), P("pass")),
        out_specs=P(("term", "pass"), None),
        check_vma=False,
    )
```

```python
import functools

import jax
import jax.numpy as jnp
from jax import lax
from jax.experimental import pallas as pl
from jax.experimental.pallas import tpu as pltpu
from jax.sharding import PartitionSpec as P

MESH = pl.DeviceIdType.MESH
ZS, XS, CS = 4, 2, 2
CHUNKS = 4
HIGHEST_VMEM = 58 * 1024 * 1024


def kernel(
    tokens_per, hid, head, out,
    tok, wts, pool, give, take,
    s_up, s_dn, r_z, s_y, r_y, s_c, r_c, s_h, r_h, s_x, r_x, s_f, r_f, s_l,
):
    y = lax.axis_index("term")
    me = lax.axis_index("pass")
    z, x, c = me // (XS * CS), (me // CS) % XS, me % CS
    block, feats = hid.shape
    feat_rows = head.shape[0]
    cols = wts.shape[2]
    rows = block // CHUNKS
    per = block // tokens_per

    def at(zz, xx, cc):
        return (zz * XS + xx) * CS + cc

    y_dev = (1 - y, me)
    x_dev = (y, at(z, 1 - x, c))
    c_dev = (y, at(z, x, 1 - c))
    up_dev = (y, at(jnp.minimum(z + 1, ZS - 1), x, c))
    dn_dev = (y, at(jnp.maximum(z - 1, 0), x, c))

    def others(do):
        for i in range(1, ZS):
            zz = lax.rem(z + i, ZS)
            for cc in range(CS):
                do(zz, cc)
        do(z, 1 - c)

    barrier = pltpu.get_barrier_semaphore()

    def hello(dev):
        pl.semaphore_signal(barrier, inc=1, device_id=dev, device_id_type=MESH)

    others(lambda zz, cc: hello((y, at(zz, x, cc))))
    hello(x_dev)
    hello(y_dev)
    pl.semaphore_wait(barrier, ZS * CS + 1)

    def remote(src, dst, send, recv, dev):
        return pltpu.make_async_remote_copy(
            src_ref=src, dst_ref=dst, send_sem=send, recv_sem=recv,
            device_id=dev, device_id_type=MESH,
        )

    def piece(f, zz, cc, k):
        return tok.at[f, zz, cc, pl.ds(k * rows, rows)]

    def own_piece(k):
        return hid.at[pl.ds(k * rows, rows)]

    def up(zz, k, src):
        return remote(src, piece(y, zz, c, k), s_up.at[zz, k], r_z.at[zz, k], up_dev)

    def down(zz, k, src):
        return remote(src, piece(y, zz, c, k), s_dn.at[zz, k], r_z.at[zz, k], dn_dev)

    def across_y(zz, k, src):
        return remote(src, piece(y, zz, c, k), s_y.at[zz, k], r_y.at[zz, k], y_dev)

    def across_c(f, zz, k, src):
        return remote(src, piece(f, zz, c, k), s_c.at[f, zz, k], r_c.at[f, zz, k], c_dev)

    def strip(zz, cc, xx):
        first = at(zz, xx, cc) * cols
        return head.at[:, pl.ds(pl.multiple_of(first, cols), cols)]

    def wts_of(p, xx):
        return wts.at[xx, pl.ds(pl.multiple_of(p * feat_rows, feat_rows), feat_rows)]

    def both_of(p):
        return wts.at[:, pl.ds(pl.multiple_of(p * feat_rows, feat_rows), feat_rows)]

    def head_to(zz, cc, xx):
        return remote(
            strip(zz, cc, xx), wts_of(me, xx),
            s_h.at[zz * CS + cc, xx], r_h.at[z * CS + c, xx], (y, at(zz, x, cc)),
        )

    def head_from(zz, cc, xx):
        ref = wts_of(at(zz, x, cc), xx)
        return remote(ref, ref, s_h.at[zz * CS + cc, xx], r_h.at[zz * CS + cc, xx], x_dev)

    def relay(zz, cc):
        ref = both_of(at(zz, x, cc))
        return remote(ref, ref, s_x.at[zz * CS + cc], r_x.at[zz * CS + cc], x_dev)

    def send_head(zz, cc):
        for xx in range(XS):
            head_to(zz, cc, xx).start()

    def pass_head(zz, cc):
        for xx in range(XS):
            head_from(zz, cc, xx).wait_recv()
        relay(zz, cc).start()

    def sides(d, do):
        def side(s, inner):
            zz = z + (1 - 2 * s) * d

            @pl.when((zz >= 0) & (zz < ZS))
            def _():
                do(zz)

            return inner

        lax.fori_loop(0, 2, side, 0)

    def pass_tokens(d, k):
        below, above = z - d, z + d

        @pl.when(below >= 0)
        def _():
            src = piece(y, below, c, k)
            up(below, k, src).wait_recv()

            @pl.when(z < ZS - 1)
            def _():
                up(below, k, src).start()

            across_y(below, k, src).start()
            across_c(y, below, k, src).start()

        @pl.when(above < ZS)
        def _():
            src = piece(y, above, c, k)
            down(above, k, src).wait_recv()

            @pl.when(z > 0)
            def _():
                down(above, k, src).start()

            across_y(above, k, src).start()
            across_c(y, above, k, src).start()

    def from_y(zz):
        def one(k, carry):
            src = piece(1 - y, zz, c, k)
            across_y(zz, k, src).wait_recv()
            across_c(1 - y, zz, k, src).start()
            return carry

        lax.fori_loop(0, CHUNKS, one, 0)

    def near_head(d):
        def both(zz):
            for cc in range(CS):
                pass_head(zz, cc)

        sides(d, both)

    local = [pltpu.make_async_copy(strip(z, c, xx), wts_of(me, xx), s_l.at[xx]) for xx in range(XS)]
    local.append(pltpu.make_async_copy(hid, tok.at[y, z, c], s_l.at[XS]))
    send_head(z, 1 - c)
    for copy in local:
        copy.start()

    def send_own(k, carry):
        @pl.when(z < ZS - 1)
        def _():
            up(z, k, own_piece(k)).start()

        @pl.when(z > 0)
        def _():
            down(z, k, own_piece(k)).start()

        across_y(z, k, own_piece(k)).start()
        across_c(y, z, k, own_piece(k)).start()

        for i in range(1, ZS):
            @pl.when(k == i * CHUNKS // ZS - 1)
            def _():
                for cc in range(CS):
                    send_head(lax.rem(z + i, ZS), cc)

        return carry

    lax.fori_loop(0, CHUNKS, send_own, 0)
    for copy in local:
        copy.wait()
    relay(z, c).start()

    def arrived(zz):
        for f in range(2):
            for k in range(CHUNKS):
                across_c(f, zz, k, piece(f, zz, 1 - c, k)).wait_recv()

    def multiply(zz, cc):
        def half(xx, carry):
            acc = jnp.dot(tok[0, zz, cc], wts[xx, pl.ds(0, feats)], preferred_element_type=jnp.float32)
            acc += jnp.dot(tok[1, zz, cc], wts[xx, pl.ds(feats, feats)], preferred_element_type=jnp.float32)
            top = jnp.max(acc.reshape(per, tokens_per, cols), axis=1)
            first = pl.multiple_of((zz * CS + cc) * per, per)
            pool[xx, pl.ds(first, per), :] = jnp.log1p(jnp.maximum(top, 0.0))
            return carry

        lax.fori_loop(0, XS, half, 0)

    hops = (ZS - 1) * CHUNKS

    def event(e, carry):
        @pl.when(e < hops)
        def _():
            pass_tokens(1 + e // CHUNKS, lax.rem(e, CHUNKS))

        @pl.when(e == 0)
        def _():
            pass_head(z, 1 - c)

        for d in range(1, ZS):
            @pl.when(e == d * CHUNKS // ZS)
            def _():
                near_head(d)

        @pl.when(e == CHUNKS)
        def _():
            from_y(z)

        @pl.when(e == hops - 6)
        def _():
            for i in range(ZS * CS):
                relay(i // CS, i % CS).wait_recv()

        j = e - (hops - 5)
        d, s = (j + 1) // 2, lax.rem(j + 1, 2)
        zz = z + (1 - 2 * s) * d

        for i in range(1, ZS):
            @pl.when(j == 2 * i - 1)
            def _():
                sides(i, from_y)

        @pl.when((j >= 0) & (zz >= 0) & (zz < ZS))
        def _():
            arrived(zz)

            def core(cc, inner):
                multiply(zz, cc)
                return inner

            lax.fori_loop(0, CS, core, 0)

        return carry

    lax.fori_loop(0, hops + 2, event, 0)

    give[...] = pool[1 - x].astype(jnp.bfloat16)
    last = remote(give, take, s_f, r_f, x_dev)
    last.start()

    def sent(zz, carry):
        for k in range(CHUNKS):
            @pl.when((zz <= z) & (z < ZS - 1))
            def _():
                up(zz, k, own_piece(k)).wait_send()

            @pl.when((zz >= z) & (z > 0))
            def _():
                down(zz, k, own_piece(k)).wait_send()

            across_y(zz, k, own_piece(k)).wait_send()
            for f in range(2):
                across_c(f, zz, k, own_piece(k)).wait_send()
        for cc in range(CS):
            relay(zz, cc).wait_send()
        return carry

    lax.fori_loop(0, ZS, sent, 0)

    def head_sent(zz, cc):
        for xx in range(XS):
            head_to(zz, cc, xx).wait_send()

    others(head_sent)
    last.wait()

    mine = pool[x].astype(jnp.bfloat16).astype(jnp.float32)
    theirs = take[...].astype(jnp.float32)
    even = jnp.where(x == 0, mine, theirs)
    odd = jnp.where(x == 0, theirs, mine)
    span = CS * per
    parts = []
    for zz in range(ZS):
        parts += [even[zz * span:(zz + 1) * span], odd[zz * span:(zz + 1) * span]]
    full = jnp.concatenate(parts, axis=0)
    peak = jnp.max(full, axis=0, keepdims=True)
    out[...] = jnp.transpose(full / (1.0 + peak)).astype(jnp.bfloat16)


def masked(hidden, lengths):
    passages = lengths.shape[0]
    tokens_per = hidden.shape[0] // passages
    allowed = jnp.arange(tokens_per, dtype=jnp.int32)[None, :] < lengths[:, None]
    return jnp.where(allowed.reshape(-1)[:, None], hidden, jnp.bfloat16(0.0))


def fused(hidden, head_weight, lengths):
    passages = lengths.shape[0]
    tokens = hidden.shape[0]
    feats = hidden.shape[1]
    feat_rows = head_weight.shape[0]
    cols = head_weight.shape[1] // (ZS * XS * CS)
    rows = ZS * CS * passages
    dma = pltpu.SemaphoreType.DMA
    return pl.pallas_call(
        functools.partial(kernel, tokens // passages),
        out_shape=jax.ShapeDtypeStruct((cols, XS * rows), jnp.bfloat16),
        in_specs=[pl.BlockSpec(memory_space=pl.ANY)] * 2,
        out_specs=pl.BlockSpec(memory_space=pltpu.VMEM),
        scratch_shapes=[
            pltpu.VMEM((2, ZS, CS, tokens, feats), jnp.bfloat16),
            pltpu.VMEM((XS, 2 * feats, cols), jnp.bfloat16),
            pltpu.VMEM((XS, rows, cols), jnp.float32),
            pltpu.VMEM((rows, cols), jnp.bfloat16),
            pltpu.VMEM((rows, cols), jnp.bfloat16),
            dma((ZS, CHUNKS)), dma((ZS, CHUNKS)), dma((ZS, CHUNKS)),
            dma((ZS, CHUNKS)), dma((ZS, CHUNKS)),
            dma((2, ZS, CHUNKS)), dma((2, ZS, CHUNKS)),
            dma((ZS * CS, XS)), dma((ZS * CS, XS)),
            dma((ZS * CS,)), dma((ZS * CS,)),
            dma, dma, dma((XS + 1,)),
        ],
        compiler_params=pltpu.CompilerParams(
            collective_id=0, has_side_effects=True, vmem_limit_bytes=HIGHEST_VMEM
        ),
        cost_estimate=pl.CostEstimate(
            flops=2 * ZS * CS * tokens * 2 * feats * XS * cols,
            bytes_accessed=2 * (tokens * feats + feat_rows * head_weight.shape[1]),
            transcendentals=0,
        ),
    )(masked(hidden, lengths), head_weight)


def general(hidden, head_weight, lengths):
    terms = lax.axis_size("term")
    owners = lax.axis_size("pass")
    passages = lengths.shape[0]
    tokens_per = hidden.shape[0] // passages
    range_cols = head_weight.shape[1] // owners
    own = lax.all_to_all(masked(hidden, lengths), "term", split_axis=0, concat_axis=1, tiled=True)
    tokens = lax.all_gather(own, "pass", axis=0, tiled=True)
    rows = lax.all_to_all(head_weight, "pass", split_axis=1, concat_axis=0, tiled=True)
    weights = lax.all_gather(rows, "term", axis=1, tiled=True)
    share = passages // terms
    logits = jnp.dot(tokens, weights, preferred_element_type=jnp.float32)
    logits = logits.reshape(owners * share, tokens_per, terms * range_cols)
    top = jnp.maximum(jnp.max(logits, axis=1), jnp.float32(0.0))
    pooled = jnp.log1p(top).astype(jnp.bfloat16)
    got = lax.all_to_all(
        pooled.reshape(owners * share, terms, range_cols), "term", split_axis=1, concat_axis=1, tiled=True
    )
    full = got.reshape(owners, share, terms, range_cols).transpose(0, 2, 1, 3)
    full = full.reshape(owners * passages, range_cols).astype(jnp.float32)
    peak = jnp.max(full, axis=0)
    return jnp.transpose((full / (1.0 + peak)[None, :]).astype(jnp.bfloat16))


def solution(mesh):
    small = mesh.shape["term"] == 2 and mesh.shape["pass"] == ZS * XS * CS
    return jax.shard_map(
        fused if small else general,
        mesh=mesh,
        in_specs=(P("pass", "term"), P("pass", "term"), P("pass")),
        out_specs=P(("term", "pass"), None),
        check_vma=False,
    )
```

```python
import functools

import jax
import jax.numpy as jnp
from jax import lax
from jax.experimental import pallas as pl
from jax.experimental.pallas import tpu as pltpu
from jax.sharding import PartitionSpec as P

MESH = pl.DeviceIdType.MESH
ZS, XS, CS = 4, 2, 2
CHUNKS = 4
HIGHEST_VMEM = 58 * 1024 * 1024


def kernel(
    tokens_per, lens, hid, head, out,
    tok, wts, pool, give, take,
    s_up, s_dn, r_z, s_y, r_y, s_c, r_c, s_h, r_h, s_x, r_x, s_f, r_f, s_l, s_t,
):
    y = lax.axis_index("term")
    me = lax.axis_index("pass")
    z, x, c = me // (XS * CS), (me // CS) % XS, me % CS
    block, feats = hid.shape
    feat_rows = head.shape[0]
    cols = wts.shape[2]
    rows = block // CHUNKS
    per = block // tokens_per

    def at(zz, xx, cc):
        return (zz * XS + xx) * CS + cc

    y_dev = (1 - y, me)
    x_dev = (y, at(z, 1 - x, c))
    c_dev = (y, at(z, x, 1 - c))
    up_dev = (y, at(jnp.minimum(z + 1, ZS - 1), x, c))
    dn_dev = (y, at(jnp.maximum(z - 1, 0), x, c))

    def others(do):
        for i in range(1, ZS):
            zz = lax.rem(z + i, ZS)
            for cc in range(CS):
                do(zz, cc)
        do(z, 1 - c)

    loads = [
        pltpu.make_async_copy(
            hid.at[pl.ds(k * rows, rows)], tok.at[y, z, c, pl.ds(k * rows, rows)], s_t.at[k]
        )
        for k in range(CHUNKS)
    ]
    for load in loads:
        load.start()

    barrier = pltpu.get_barrier_semaphore()

    def hello(dev):
        pl.semaphore_signal(barrier, inc=1, device_id=dev, device_id_type=MESH)

    others(lambda zz, cc: hello((y, at(zz, x, cc))))
    hello(x_dev)
    hello(y_dev)
    pl.semaphore_wait(barrier, ZS * CS + 1)

    def remote(src, dst, send, recv, dev):
        return pltpu.make_async_remote_copy(
            src_ref=src, dst_ref=dst, send_sem=send, recv_sem=recv,
            device_id=dev, device_id_type=MESH,
        )

    def piece(f, zz, cc, k):
        return tok.at[f, zz, cc, pl.ds(k * rows, rows)]

    def own_piece(k):
        return piece(y, z, c, k)

    def up(zz, k, src):
        return remote(src, piece(y, zz, c, k), s_up.at[zz, k], r_z.at[zz, k], up_dev)

    def down(zz, k, src):
        return remote(src, piece(y, zz, c, k), s_dn.at[zz, k], r_z.at[zz, k], dn_dev)

    def across_y(zz, k, src):
        return remote(src, piece(y, zz, c, k), s_y.at[zz, k], r_y.at[zz, k], y_dev)

    def across_c(f, zz, k, src):
        return remote(src, piece(f, zz, c, k), s_c.at[f, zz, k], r_c.at[f, zz, k], c_dev)

    def strip(zz, cc, xx):
        first = at(zz, xx, cc) * cols
        return head.at[:, pl.ds(pl.multiple_of(first, cols), cols)]

    def wts_of(p, xx):
        return wts.at[xx, pl.ds(pl.multiple_of(p * feat_rows, feat_rows), feat_rows)]

    def both_of(p):
        return wts.at[:, pl.ds(pl.multiple_of(p * feat_rows, feat_rows), feat_rows)]

    def head_to(zz, cc, xx):
        return remote(
            strip(zz, cc, xx), wts_of(me, xx),
            s_h.at[zz * CS + cc, xx], r_h.at[z * CS + c, xx], (y, at(zz, x, cc)),
        )

    def head_from(zz, cc, xx):
        ref = wts_of(at(zz, x, cc), xx)
        return remote(ref, ref, s_h.at[zz * CS + cc, xx], r_h.at[zz * CS + cc, xx], x_dev)

    def relay(zz, cc):
        ref = both_of(at(zz, x, cc))
        return remote(ref, ref, s_x.at[zz * CS + cc], r_x.at[zz * CS + cc], x_dev)

    def send_head(zz, cc):
        for xx in range(XS):
            head_to(zz, cc, xx).start()

    def pass_head(zz, cc):
        for xx in range(XS):
            head_from(zz, cc, xx).wait_recv()
        relay(zz, cc).start()

    def sides(d, do):
        def side(s, inner):
            zz = z + (1 - 2 * s) * d

            @pl.when((zz >= 0) & (zz < ZS))
            def _():
                do(zz)

            return inner

        lax.fori_loop(0, 2, side, 0)

    def pass_tokens(d, k):
        below, above = z - d, z + d

        @pl.when(below >= 0)
        def _():
            src = piece(y, below, c, k)
            up(below, k, src).wait_recv()

            @pl.when(z < ZS - 1)
            def _():
                up(below, k, src).start()

            across_y(below, k, src).start()
            across_c(y, below, k, src).start()

        @pl.when(above < ZS)
        def _():
            src = piece(y, above, c, k)
            down(above, k, src).wait_recv()

            @pl.when(z > 0)
            def _():
                down(above, k, src).start()

            across_y(above, k, src).start()
            across_c(y, above, k, src).start()

    def from_y(zz):
        def one(k, carry):
            src = piece(1 - y, zz, c, k)
            across_y(zz, k, src).wait_recv()
            across_c(1 - y, zz, k, src).start()
            return carry

        lax.fori_loop(0, CHUNKS, one, 0)

    def near_head(d):
        def both(zz):
            for cc in range(CS):
                pass_head(zz, cc)

        sides(d, both)

    local = [pltpu.make_async_copy(strip(z, c, xx), wts_of(me, xx), s_l.at[xx]) for xx in range(XS)]
    send_head(z, 1 - c)
    for copy in local:
        copy.start()

    slots = lax.broadcasted_iota(jnp.int32, (tokens_per, feats), 0)
    for k in range(CHUNKS):
        loads[k].wait()
        for i in range(k * rows // tokens_per, (k + 1) * rows // tokens_per):
            own = (y, z, c, pl.ds(i * tokens_per, tokens_per))
            kept = jnp.where(slots < lens[i], tok[own].astype(jnp.float32), 0.0)
            tok[own] = kept.astype(jnp.bfloat16)

    def send_own(k, carry):
        @pl.when(z < ZS - 1)
        def _():
            up(z, k, own_piece(k)).start()

        @pl.when(z > 0)
        def _():
            down(z, k, own_piece(k)).start()

        across_y(z, k, own_piece(k)).start()
        across_c(y, z, k, own_piece(k)).start()

        for i in range(1, ZS):
            @pl.when(k == i * CHUNKS // ZS - 1)
            def _():
                for cc in range(CS):
                    send_head(lax.rem(z + i, ZS), cc)

        return carry

    lax.fori_loop(0, CHUNKS, send_own, 0)
    for copy in local:
        copy.wait()
    relay(z, c).start()

    def arrived(zz, h):
        for f in range(2):
            for k in range(CHUNKS // 2):
                at_k = h * (CHUNKS // 2) + k
                across_c(f, zz, at_k, piece(f, zz, 1 - c, at_k)).wait_recv()

    def multiply(zz, h):
        tall = block // 2

        def part(i, carry):
            cc, xx = i // XS, lax.rem(i, XS)
            span = pl.ds(pl.multiple_of(h * tall, tall), tall)
            acc = jnp.dot(tok[0, zz, cc, span], wts[xx, pl.ds(0, feats)], preferred_element_type=jnp.float32)
            acc += jnp.dot(tok[1, zz, cc, span], wts[xx, pl.ds(feats, feats)], preferred_element_type=jnp.float32)
            top = jnp.max(acc.reshape(per // 2, tokens_per, cols), axis=1)
            top = jnp.log1p(jnp.maximum(top, 0.0))
            both = jnp.concatenate([top, top], axis=0)
            place = lax.broadcasted_iota(jnp.int32, both.shape, 0) // (per // 2)
            first = pl.multiple_of((zz * CS + cc) * per, per)
            old = jnp.where(h == 0, 0.0, pool[xx, pl.ds(first, per), :])
            pool[xx, pl.ds(first, per), :] = jnp.where(place == h, both, old)
            return carry

        lax.fori_loop(0, CS * XS, part, 0)

    hops = (ZS - 1) * CHUNKS

    def event(e, carry):
        @pl.when(e < hops)
        def _():
            pass_tokens(1 + e // CHUNKS, lax.rem(e, CHUNKS))

        @pl.when(e == 0)
        def _():
            pass_head(z, 1 - c)

        for d in range(1, ZS):
            @pl.when(e == d * CHUNKS // ZS)
            def _():
                near_head(d)

        @pl.when(e == CHUNKS)
        def _():
            from_y(z)

        @pl.when(e == lead - CHUNKS // 4)
        def _():
            for i in range(ZS * CS):
                relay(i // CS, i % CS).wait_recv()

        j = (e - lead) // (CHUNKS // 4)
        low = z < ZS // 2
        near = jnp.where(z == 0, 1, z - 1)
        far = jnp.where(z == ZS - 1, -1, z + 1)
        zz = jnp.where(j == 0, z, jnp.where(j == 1, near, jnp.where(j == 2, far, jnp.where(
            j == 3, jnp.where(low, z + 2, z - 2), jnp.where(low, z + 3, z - 3)))))
        there = (j >= 0) & (j < 6) & (lax.rem(e - lead, CHUNKS // 4) == 0) & (zz >= 0) & (zz < ZS)
        there = there & ((j != 2) | (z > 0))
        begin = jnp.where(j == 5, 1, 0)
        end = jnp.where(j == 4, 1, 2)

        @pl.when(there)
        def _():
            def halves(h, inner):
                @pl.when(j > 0)
                def _():
                    for k in range(CHUNKS // 2):
                        at_k = h * (CHUNKS // 2) + k
                        src = piece(1 - y, zz, c, at_k)
                        across_y(zz, at_k, src).wait_recv()
                        across_c(1 - y, zz, at_k, src).start()

                arrived(zz, h)
                multiply(zz, h)
                return inner

            lax.fori_loop(begin, end, halves, 0)

        return carry

    lead = hops - 5 * CHUNKS // 4
    lax.fori_loop(0, hops + CHUNKS // 4, event, 0)

    give[...] = pool[1 - x].astype(jnp.bfloat16)
    last = remote(give, take, s_f, r_f, x_dev)
    last.start()

    def sent(zz, carry):
        for k in range(CHUNKS):
            @pl.when((zz <= z) & (z < ZS - 1))
            def _():
                up(zz, k, own_piece(k)).wait_send()

            @pl.when((zz >= z) & (z > 0))
            def _():
                down(zz, k, own_piece(k)).wait_send()

            across_y(zz, k, own_piece(k)).wait_send()
            for f in range(2):
                across_c(f, zz, k, own_piece(k)).wait_send()
        for cc in range(CS):
            relay(zz, cc).wait_send()
        return carry

    lax.fori_loop(0, ZS, sent, 0)

    def head_sent(zz, cc):
        for xx in range(XS):
            head_to(zz, cc, xx).wait_send()

    others(head_sent)
    last.wait()

    mine = pool[x].astype(jnp.bfloat16).astype(jnp.float32)
    theirs = take[...].astype(jnp.float32)
    even = jnp.where(x == 0, mine, theirs)
    odd = jnp.where(x == 0, theirs, mine)
    span = CS * per
    parts = []
    for zz in range(ZS):
        parts += [even[zz * span:(zz + 1) * span], odd[zz * span:(zz + 1) * span]]
    full = jnp.concatenate(parts, axis=0)
    peak = jnp.max(full, axis=0, keepdims=True)
    out[...] = jnp.transpose(full / (1.0 + peak)).astype(jnp.bfloat16)


def masked(hidden, lengths):
    passages = lengths.shape[0]
    tokens_per = hidden.shape[0] // passages
    allowed = jnp.arange(tokens_per, dtype=jnp.int32)[None, :] < lengths[:, None]
    return jnp.where(allowed.reshape(-1)[:, None], hidden, jnp.bfloat16(0.0))


def fused(hidden, head_weight, lengths):
    passages = lengths.shape[0]
    tokens = hidden.shape[0]
    feats = hidden.shape[1]
    feat_rows = head_weight.shape[0]
    cols = head_weight.shape[1] // (ZS * XS * CS)
    rows = ZS * CS * passages
    dma = pltpu.SemaphoreType.DMA
    return pl.pallas_call(
        functools.partial(kernel, tokens // passages),
        out_shape=jax.ShapeDtypeStruct((cols, XS * rows), jnp.bfloat16),
        in_specs=[pl.BlockSpec(memory_space=pltpu.SMEM)] + [pl.BlockSpec(memory_space=pl.ANY)] * 2,
        out_specs=pl.BlockSpec(memory_space=pltpu.VMEM),
        scratch_shapes=[
            pltpu.VMEM((2, ZS, CS, tokens, feats), jnp.bfloat16),
            pltpu.VMEM((XS, 2 * feats, cols), jnp.bfloat16),
            pltpu.VMEM((XS, rows, cols), jnp.float32),
            pltpu.VMEM((rows, cols), jnp.bfloat16),
            pltpu.VMEM((rows, cols), jnp.bfloat16),
            dma((ZS, CHUNKS)), dma((ZS, CHUNKS)), dma((ZS, CHUNKS)),
            dma((ZS, CHUNKS)), dma((ZS, CHUNKS)),
            dma((2, ZS, CHUNKS)), dma((2, ZS, CHUNKS)),
            dma((ZS * CS, XS)), dma((ZS * CS, XS)),
            dma((ZS * CS,)), dma((ZS * CS,)),
            dma, dma, dma((XS,)), dma((CHUNKS,)),
        ],
        compiler_params=pltpu.CompilerParams(
            collective_id=0, has_side_effects=True, vmem_limit_bytes=HIGHEST_VMEM
        ),
        cost_estimate=pl.CostEstimate(
            flops=2 * ZS * CS * tokens * 2 * feats * XS * cols,
            bytes_accessed=2 * (tokens * feats + feat_rows * head_weight.shape[1]),
            transcendentals=0,
        ),
    )(lengths, hidden, head_weight)


def general(hidden, head_weight, lengths):
    terms = lax.axis_size("term")
    owners = lax.axis_size("pass")
    passages = lengths.shape[0]
    tokens_per = hidden.shape[0] // passages
    range_cols = head_weight.shape[1] // owners
    own = lax.all_to_all(masked(hidden, lengths), "term", split_axis=0, concat_axis=1, tiled=True)
    tokens = lax.all_gather(own, "pass", axis=0, tiled=True)
    rows = lax.all_to_all(head_weight, "pass", split_axis=1, concat_axis=0, tiled=True)
    weights = lax.all_gather(rows, "term", axis=1, tiled=True)
    share = passages // terms
    logits = jnp.dot(tokens, weights, preferred_element_type=jnp.float32)
    logits = logits.reshape(owners * share, tokens_per, terms * range_cols)
    top = jnp.maximum(jnp.max(logits, axis=1), jnp.float32(0.0))
    pooled = jnp.log1p(top).astype(jnp.bfloat16)
    got = lax.all_to_all(
        pooled.reshape(owners * share, terms, range_cols), "term", split_axis=1, concat_axis=1, tiled=True
    )
    full = got.reshape(owners, share, terms, range_cols).transpose(0, 2, 1, 3)
    full = full.reshape(owners * passages, range_cols).astype(jnp.float32)
    peak = jnp.max(full, axis=0)
    return jnp.transpose((full / (1.0 + peak)[None, :]).astype(jnp.bfloat16))


def solution(mesh):
    small = mesh.shape["term"] == 2 and mesh.shape["pass"] == ZS * XS * CS
    return jax.shard_map(
        fused if small else general,
        mesh=mesh,
        in_specs=(P("pass", "term"), P("pass", "term"), P("pass")),
        out_specs=P(("term", "pass"), None),
        check_vma=False,
    )
```

```python
import functools

import jax
import jax.numpy as jnp
from jax import lax
from jax.experimental import pallas as pl
from jax.experimental.pallas import tpu as pltpu
from jax.sharding import PartitionSpec as P

MESH = pl.DeviceIdType.MESH
ZS, XS, CS = 4, 2, 2
CHUNKS = 4
HIGHEST_VMEM = 58 * 1024 * 1024


def kernel(
    tokens_per, lens, hid, head, out,
    tok, wts, pool, give, take,
    s_up, s_dn, r_z, s_y, r_y, s_c, r_c, s_h, r_h, s_x, r_x, s_f, r_f, s_l, s_t,
):
    y = lax.axis_index("term")
    me = lax.axis_index("pass")
    z, x, c = me // (XS * CS), (me // CS) % XS, me % CS
    block, feats = hid.shape
    feat_rows = head.shape[0]
    cols = wts.shape[2]
    rows = block // CHUNKS
    per = block // tokens_per

    def at(zz, xx, cc):
        return (zz * XS + xx) * CS + cc

    y_dev = (1 - y, me)
    x_dev = (y, at(z, 1 - x, c))
    c_dev = (y, at(z, x, 1 - c))
    up_dev = (y, at(jnp.minimum(z + 1, ZS - 1), x, c))
    dn_dev = (y, at(jnp.maximum(z - 1, 0), x, c))

    def others(do):
        for i in range(1, ZS):
            zz = lax.rem(z + i, ZS)
            for cc in range(CS):
                do(zz, cc)
        do(z, 1 - c)

    loads = [
        pltpu.make_async_copy(
            hid.at[pl.ds(k * rows, rows)], tok.at[y, z, c, pl.ds(k * rows, rows)], s_t.at[k]
        )
        for k in range(CHUNKS)
    ]
    for load in loads:
        load.start()

    barrier = pltpu.get_barrier_semaphore()

    def hello(dev):
        pl.semaphore_signal(barrier, inc=1, device_id=dev, device_id_type=MESH)

    others(lambda zz, cc: hello((y, at(zz, x, cc))))
    hello(x_dev)
    hello(y_dev)
    pl.semaphore_wait(barrier, ZS * CS + 1)

    def remote(src, dst, send, recv, dev):
        return pltpu.make_async_remote_copy(
            src_ref=src, dst_ref=dst, send_sem=send, recv_sem=recv,
            device_id=dev, device_id_type=MESH,
        )

    def piece(f, zz, cc, k):
        return tok.at[f, zz, cc, pl.ds(k * rows, rows)]

    def own_piece(k):
        return piece(y, z, c, k)

    def up(zz, k, src):
        return remote(src, piece(y, zz, c, k), s_up.at[zz, k], r_z.at[zz, k], up_dev)

    def down(zz, k, src):
        return remote(src, piece(y, zz, c, k), s_dn.at[zz, k], r_z.at[zz, k], dn_dev)

    def across_y(zz, k, src):
        return remote(src, piece(y, zz, c, k), s_y.at[zz, k], r_y.at[zz, k], y_dev)

    def across_c(f, zz, k, src):
        return remote(src, piece(f, zz, c, k), s_c.at[f, zz, k], r_c.at[f, zz, k], c_dev)

    def strip(zz, cc, xx):
        first = at(zz, xx, cc) * cols
        return head.at[:, pl.ds(pl.multiple_of(first, cols), cols)]

    def wts_of(p, xx):
        return wts.at[xx, pl.ds(pl.multiple_of(p * feat_rows, feat_rows), feat_rows)]

    def both_of(p):
        return wts.at[:, pl.ds(pl.multiple_of(p * feat_rows, feat_rows), feat_rows)]

    def head_to(zz, cc, xx):
        return remote(
            strip(zz, cc, xx), wts_of(me, xx),
            s_h.at[zz * CS + cc, xx], r_h.at[z * CS + c, xx], (y, at(zz, x, cc)),
        )

    def head_from(zz, cc, xx):
        ref = wts_of(at(zz, x, cc), xx)
        return remote(ref, ref, s_h.at[zz * CS + cc, xx], r_h.at[zz * CS + cc, xx], x_dev)

    def relay(zz, cc):
        ref = both_of(at(zz, x, cc))
        return remote(ref, ref, s_x.at[zz * CS + cc], r_x.at[zz * CS + cc], x_dev)

    def send_head(zz, cc):
        for xx in range(XS):
            head_to(zz, cc, xx).start()

    def pass_head(zz, cc):
        for xx in range(XS):
            head_from(zz, cc, xx).wait_recv()
        relay(zz, cc).start()

    def sides(d, do):
        def side(s, inner):
            zz = z + (1 - 2 * s) * d

            @pl.when((zz >= 0) & (zz < ZS))
            def _():
                do(zz)

            return inner

        lax.fori_loop(0, 2, side, 0)

    def pass_tokens(d, k):
        below, above = z - d, z + d

        @pl.when(below >= 0)
        def _():
            src = piece(y, below, c, k)
            up(below, k, src).wait_recv()

            @pl.when(z < ZS - 1)
            def _():
                up(below, k, src).start()

            across_y(below, k, src).start()
            across_c(y, below, k, src).start()

        @pl.when(above < ZS)
        def _():
            src = piece(y, above, c, k)
            down(above, k, src).wait_recv()

            @pl.when(z > 0)
            def _():
                down(above, k, src).start()

            across_y(above, k, src).start()
            across_c(y, above, k, src).start()

    def from_y(zz):
        def one(k, carry):
            src = piece(1 - y, zz, c, k)
            across_y(zz, k, src).wait_recv()
            across_c(1 - y, zz, k, src).start()
            return carry

        lax.fori_loop(0, CHUNKS, one, 0)

    def near_head(d):
        def both(zz):
            for cc in range(CS):
                pass_head(zz, cc)

        sides(d, both)

    local = [pltpu.make_async_copy(strip(z, c, xx), wts_of(me, xx), s_l.at[xx]) for xx in range(XS)]
    send_head(z, 1 - c)
    for copy in local:
        copy.start()

    slots = lax.broadcasted_iota(jnp.int32, (tokens_per, feats), 0)
    for k in range(CHUNKS):
        loads[k].wait()
        for i in range(k * rows // tokens_per, (k + 1) * rows // tokens_per):
            own = (y, z, c, pl.ds(i * tokens_per, tokens_per))
            kept = jnp.where(slots < lens[i], tok[own].astype(jnp.float32), 0.0)
            tok[own] = kept.astype(jnp.bfloat16)

    def send_own(k, carry):
        @pl.when(z < ZS - 1)
        def _():
            up(z, k, own_piece(k)).start()

        @pl.when(z > 0)
        def _():
            down(z, k, own_piece(k)).start()

        across_y(z, k, own_piece(k)).start()
        across_c(y, z, k, own_piece(k)).start()

        for i in range(1, ZS):
            @pl.when(k == i * CHUNKS // ZS - 1)
            def _():
                for cc in range(CS):
                    send_head(lax.rem(z + i, ZS), cc)

        return carry

    lax.fori_loop(0, CHUNKS, send_own, 0)
    for copy in local:
        copy.wait()
    relay(z, c).start()

    def arrived(zz, h):
        for f in range(2):
            for k in range(CHUNKS // 2):
                at_k = h * (CHUNKS // 2) + k
                across_c(f, zz, at_k, piece(f, zz, 1 - c, at_k)).wait_recv()

    def multiply(zz, h):
        tall = block // 2

        def part(i, carry):
            cc, xx = i // XS, lax.rem(i, XS)
            span = pl.ds(pl.multiple_of(h * tall, tall), tall)
            acc = jnp.dot(tok[0, zz, cc, span], wts[xx, pl.ds(0, feats)], preferred_element_type=jnp.float32)
            acc += jnp.dot(tok[1, zz, cc, span], wts[xx, pl.ds(feats, feats)], preferred_element_type=jnp.float32)
            top = jnp.max(acc.reshape(per // 2, tokens_per, cols), axis=1)
            top = jnp.log1p(jnp.maximum(top, 0.0))
            both = jnp.concatenate([top, top], axis=0)
            place = lax.broadcasted_iota(jnp.int32, both.shape, 0) // (per // 2)
            first = pl.multiple_of((zz * CS + cc) * per, per)
            old = jnp.where(h == 0, 0.0, pool[xx, pl.ds(first, per), :])
            pool[xx, pl.ds(first, per), :] = jnp.where(place == h, both, old)
            return carry

        lax.fori_loop(0, CS * XS, part, 0)

    hops = (ZS - 1) * CHUNKS

    def event(e, carry):
        @pl.when(e < hops)
        def _():
            pass_tokens(1 + e // CHUNKS, lax.rem(e, CHUNKS))

        @pl.when(e == 0)
        def _():
            pass_head(z, 1 - c)

        for d in range(1, ZS):
            @pl.when(e == d * CHUNKS // ZS)
            def _():
                near_head(d)

        @pl.when(e == CHUNKS)
        def _():
            from_y(z)

        @pl.when(e == lead)
        def _():
            for i in range(ZS * CS):
                relay(i // CS, i % CS).wait_recv()

        j = e - lead
        j = jnp.where(j >= 5, j - 2, jnp.where(j >= 3, -1, j))
        low = z < ZS // 2
        near = jnp.where(z == 0, 1, z - 1)
        far = jnp.where(z == ZS - 1, -1, z + 1)
        zz = jnp.where(j == 0, z, jnp.where(j == 1, near, jnp.where(j == 2, far, jnp.where(
            j == 3, jnp.where(low, z + 2, z - 2), jnp.where(low, z + 3, z - 3)))))
        there = (j >= 0) & (j < 6) & (zz >= 0) & (zz < ZS)
        there = there & ((j != 2) | (z > 0))
        begin = jnp.where(j == 5, 1, 0)
        end = jnp.where(j == 4, 1, 2)

        @pl.when(there)
        def _():
            def halves(h, inner):
                @pl.when(j > 0)
                def _():
                    for k in range(CHUNKS // 2):
                        at_k = h * (CHUNKS // 2) + k
                        src = piece(1 - y, zz, c, at_k)
                        across_y(zz, at_k, src).wait_recv()
                        across_c(1 - y, zz, at_k, src).start()

                arrived(zz, h)
                multiply(zz, h)
                return inner

            lax.fori_loop(begin, end, halves, 0)

        return carry

    lead = hops - 7
    lax.fori_loop(0, hops + 1, event, 0)

    give[...] = pool[1 - x].astype(jnp.bfloat16)
    last = remote(give, take, s_f, r_f, x_dev)
    last.start()

    def sent(zz, carry):
        for k in range(CHUNKS):
            @pl.when((zz <= z) & (z < ZS - 1))
            def _():
                up(zz, k, own_piece(k)).wait_send()

            @pl.when((zz >= z) & (z > 0))
            def _():
                down(zz, k, own_piece(k)).wait_send()

            across_y(zz, k, own_piece(k)).wait_send()
            for f in range(2):
                across_c(f, zz, k, own_piece(k)).wait_send()
        for cc in range(CS):
            relay(zz, cc).wait_send()
        return carry

    lax.fori_loop(0, ZS, sent, 0)

    def head_sent(zz, cc):
        for xx in range(XS):
            head_to(zz, cc, xx).wait_send()

    others(head_sent)
    last.wait()

    mine = pool[x].astype(jnp.bfloat16).astype(jnp.float32)
    theirs = take[...].astype(jnp.float32)
    even = jnp.where(x == 0, mine, theirs)
    odd = jnp.where(x == 0, theirs, mine)
    span = CS * per
    parts = []
    for zz in range(ZS):
        parts += [even[zz * span:(zz + 1) * span], odd[zz * span:(zz + 1) * span]]
    full = jnp.concatenate(parts, axis=0)
    peak = jnp.max(full, axis=0, keepdims=True)
    out[...] = jnp.transpose(full / (1.0 + peak)).astype(jnp.bfloat16)


def masked(hidden, lengths):
    passages = lengths.shape[0]
    tokens_per = hidden.shape[0] // passages
    allowed = jnp.arange(tokens_per, dtype=jnp.int32)[None, :] < lengths[:, None]
    return jnp.where(allowed.reshape(-1)[:, None], hidden, jnp.bfloat16(0.0))


def fused(hidden, head_weight, lengths):
    passages = lengths.shape[0]
    tokens = hidden.shape[0]
    feats = hidden.shape[1]
    feat_rows = head_weight.shape[0]
    cols = head_weight.shape[1] // (ZS * XS * CS)
    rows = ZS * CS * passages
    dma = pltpu.SemaphoreType.DMA
    return pl.pallas_call(
        functools.partial(kernel, tokens // passages),
        out_shape=jax.ShapeDtypeStruct((cols, XS * rows), jnp.bfloat16),
        in_specs=[pl.BlockSpec(memory_space=pltpu.SMEM)] + [pl.BlockSpec(memory_space=pl.ANY)] * 2,
        out_specs=pl.BlockSpec(memory_space=pltpu.VMEM),
        scratch_shapes=[
            pltpu.VMEM((2, ZS, CS, tokens, feats), jnp.bfloat16),
            pltpu.VMEM((XS, 2 * feats, cols), jnp.bfloat16),
            pltpu.VMEM((XS, rows, cols), jnp.float32),
            pltpu.VMEM((rows, cols), jnp.bfloat16),
            pltpu.VMEM((rows, cols), jnp.bfloat16),
            dma((ZS, CHUNKS)), dma((ZS, CHUNKS)), dma((ZS, CHUNKS)),
            dma((ZS, CHUNKS)), dma((ZS, CHUNKS)),
            dma((2, ZS, CHUNKS)), dma((2, ZS, CHUNKS)),
            dma((ZS * CS, XS)), dma((ZS * CS, XS)),
            dma((ZS * CS,)), dma((ZS * CS,)),
            dma, dma, dma((XS,)), dma((CHUNKS,)),
        ],
        compiler_params=pltpu.CompilerParams(
            collective_id=0, has_side_effects=True, vmem_limit_bytes=HIGHEST_VMEM
        ),
        cost_estimate=pl.CostEstimate(
            flops=2 * ZS * CS * tokens * 2 * feats * XS * cols,
            bytes_accessed=2 * (tokens * feats + feat_rows * head_weight.shape[1]),
            transcendentals=0,
        ),
    )(lengths, hidden, head_weight)


def general(hidden, head_weight, lengths):
    terms = lax.axis_size("term")
    owners = lax.axis_size("pass")
    passages = lengths.shape[0]
    tokens_per = hidden.shape[0] // passages
    range_cols = head_weight.shape[1] // owners
    own = lax.all_to_all(masked(hidden, lengths), "term", split_axis=0, concat_axis=1, tiled=True)
    tokens = lax.all_gather(own, "pass", axis=0, tiled=True)
    rows = lax.all_to_all(head_weight, "pass", split_axis=1, concat_axis=0, tiled=True)
    weights = lax.all_gather(rows, "term", axis=1, tiled=True)
    share = passages // terms
    logits = jnp.dot(tokens, weights, preferred_element_type=jnp.float32)
    logits = logits.reshape(owners * share, tokens_per, terms * range_cols)
    top = jnp.maximum(jnp.max(logits, axis=1), jnp.float32(0.0))
    pooled = jnp.log1p(top).astype(jnp.bfloat16)
    got = lax.all_to_all(
        pooled.reshape(owners * share, terms, range_cols), "term", split_axis=1, concat_axis=1, tiled=True
    )
    full = got.reshape(owners, share, terms, range_cols).transpose(0, 2, 1, 3)
    full = full.reshape(owners * passages, range_cols).astype(jnp.float32)
    peak = jnp.max(full, axis=0)
    return jnp.transpose((full / (1.0 + peak)[None, :]).astype(jnp.bfloat16))


def solution(mesh):
    small = mesh.shape["term"] == 2 and mesh.shape["pass"] == ZS * XS * CS
    return jax.shard_map(
        fused if small else general,
        mesh=mesh,
        in_specs=(P("pass", "term"), P("pass", "term"), P("pass")),
        out_specs=P(("term", "pass"), None),
        check_vma=False,
    )
```

```python
import functools

import jax
import jax.numpy as jnp
from jax import lax
from jax.experimental import pallas as pl
from jax.experimental.pallas import tpu as pltpu
from jax.sharding import PartitionSpec as P

MESH = pl.DeviceIdType.MESH
ZS, XS, CS = 4, 2, 2
CHUNKS = 4
HIGHEST_VMEM = 58 * 1024 * 1024


def kernel(
    tokens_per, lens, hid, head, out,
    tok, wts, pool, give, take,
    s_up, s_dn, r_z, s_y, r_y, s_c, r_c, s_h, r_h, s_x, r_x, s_f, r_f, s_l, s_t,
):
    y = lax.axis_index("term")
    me = lax.axis_index("pass")
    z, x, c = me // (XS * CS), (me // CS) % XS, me % CS
    block, feats = hid.shape
    feat_rows = head.shape[0]
    cols = wts.shape[2]
    rows = block // CHUNKS
    per = block // tokens_per

    def at(zz, xx, cc):
        return (zz * XS + xx) * CS + cc

    y_dev = (1 - y, me)
    x_dev = (y, at(z, 1 - x, c))
    c_dev = (y, at(z, x, 1 - c))
    up_dev = (y, at(jnp.minimum(z + 1, ZS - 1), x, c))
    dn_dev = (y, at(jnp.maximum(z - 1, 0), x, c))

    def others(do):
        for i in range(1, ZS):
            zz = lax.rem(z + i, ZS)
            for cc in range(CS):
                do(zz, cc)
        do(z, 1 - c)

    loads = [
        pltpu.make_async_copy(
            hid.at[pl.ds(k * rows, rows)], tok.at[y, z, c, pl.ds(k * rows, rows)], s_t.at[k]
        )
        for k in range(CHUNKS)
    ]
    for load in loads:
        load.start()

    barrier = pltpu.get_barrier_semaphore()

    def hello(dev):
        pl.semaphore_signal(barrier, inc=1, device_id=dev, device_id_type=MESH)

    others(lambda zz, cc: hello((y, at(zz, x, cc))))
    hello(x_dev)
    hello(y_dev)
    pl.semaphore_wait(barrier, ZS * CS + 1)

    def remote(src, dst, send, recv, dev):
        return pltpu.make_async_remote_copy(
            src_ref=src, dst_ref=dst, send_sem=send, recv_sem=recv,
            device_id=dev, device_id_type=MESH,
        )

    def piece(f, zz, cc, k):
        return tok.at[f, zz, cc, pl.ds(k * rows, rows)]

    def own_piece(k):
        return piece(y, z, c, k)

    def up(zz, k, src):
        return remote(src, piece(y, zz, c, k), s_up.at[zz, k], r_z.at[zz, k], up_dev)

    def down(zz, k, src):
        return remote(src, piece(y, zz, c, k), s_dn.at[zz, k], r_z.at[zz, k], dn_dev)

    def across_y(zz, k, src):
        return remote(src, piece(y, zz, c, k), s_y.at[zz, k], r_y.at[zz, k], y_dev)

    def across_c(f, zz, k, src):
        return remote(src, piece(f, zz, c, k), s_c.at[f, zz, k], r_c.at[f, zz, k], c_dev)

    def strip(zz, cc, xx):
        first = at(zz, xx, cc) * cols
        return head.at[:, pl.ds(pl.multiple_of(first, cols), cols)]

    def wts_of(p, xx):
        return wts.at[xx, pl.ds(pl.multiple_of(p * feat_rows, feat_rows), feat_rows)]

    def both_of(p):
        return wts.at[:, pl.ds(pl.multiple_of(p * feat_rows, feat_rows), feat_rows)]

    def head_to(zz, cc, xx):
        return remote(
            strip(zz, cc, xx), wts_of(me, xx),
            s_h.at[zz * CS + cc, xx], r_h.at[z * CS + c, xx], (y, at(zz, x, cc)),
        )

    def head_from(zz, cc, xx):
        ref = wts_of(at(zz, x, cc), xx)
        return remote(ref, ref, s_h.at[zz * CS + cc, xx], r_h.at[zz * CS + cc, xx], x_dev)

    def relay(zz, cc):
        ref = both_of(at(zz, x, cc))
        return remote(ref, ref, s_x.at[zz * CS + cc], r_x.at[zz * CS + cc], x_dev)

    def send_head(zz, cc):
        for xx in range(XS):
            head_to(zz, cc, xx).start()

    def pass_head(zz, cc):
        for xx in range(XS):
            head_from(zz, cc, xx).wait_recv()
        relay(zz, cc).start()

    def sides(d, do):
        def side(s, inner):
            zz = z + (1 - 2 * s) * d

            @pl.when((zz >= 0) & (zz < ZS))
            def _():
                do(zz)

            return inner

        lax.fori_loop(0, 2, side, 0)

    def pass_tokens(d, k):
        below, above = z - d, z + d

        @pl.when(below >= 0)
        def _():
            src = piece(y, below, c, k)
            up(below, k, src).wait_recv()

            @pl.when(z < ZS - 1)
            def _():
                up(below, k, src).start()

            across_y(below, k, src).start()
            across_c(y, below, k, src).start()

        @pl.when(above < ZS)
        def _():
            src = piece(y, above, c, k)
            down(above, k, src).wait_recv()

            @pl.when(z > 0)
            def _():
                down(above, k, src).start()

            across_y(above, k, src).start()
            across_c(y, above, k, src).start()

    def from_y(zz):
        def one(k, carry):
            src = piece(1 - y, zz, c, k)
            across_y(zz, k, src).wait_recv()
            across_c(1 - y, zz, k, src).start()
            return carry

        lax.fori_loop(0, CHUNKS, one, 0)

    def near_head(d):
        def both(zz):
            for cc in range(CS):
                pass_head(zz, cc)

        sides(d, both)

    local = [pltpu.make_async_copy(strip(z, c, xx), wts_of(me, xx), s_l.at[xx]) for xx in range(XS)]
    send_head(z, 1 - c)
    for copy in local:
        copy.start()

    slots = lax.broadcasted_iota(jnp.int32, (tokens_per, feats), 0)
    for k in range(CHUNKS):
        loads[k].wait()
        for i in range(k * rows // tokens_per, (k + 1) * rows // tokens_per):
            own = (y, z, c, pl.ds(i * tokens_per, tokens_per))
            kept = jnp.where(slots < lens[i], tok[own].astype(jnp.float32), 0.0)
            tok[own] = kept.astype(jnp.bfloat16)

    def send_own(k, carry):
        @pl.when(z < ZS - 1)
        def _():
            up(z, k, own_piece(k)).start()

        @pl.when(z > 0)
        def _():
            down(z, k, own_piece(k)).start()

        across_y(z, k, own_piece(k)).start()
        across_c(y, z, k, own_piece(k)).start()

        for i in range(1, ZS):
            @pl.when(k == i * CHUNKS // ZS - 1)
            def _():
                def strips(zz):
                    for cc in range(CS):
                        send_head(zz, cc)

                sides(i, strips)

        return carry

    lax.fori_loop(0, CHUNKS, send_own, 0)
    for copy in local:
        copy.wait()
    relay(z, c).start()

    def arrived(zz, h):
        for f in range(2):
            for k in range(CHUNKS // 2):
                at_k = h * (CHUNKS // 2) + k
                across_c(f, zz, at_k, piece(f, zz, 1 - c, at_k)).wait_recv()

    def multiply(zz, h):
        tall = block // 2

        def part(i, carry):
            cc, xx = i // XS, lax.rem(i, XS)
            span = pl.ds(pl.multiple_of(h * tall, tall), tall)
            acc = jnp.dot(tok[0, zz, cc, span], wts[xx, pl.ds(0, feats)], preferred_element_type=jnp.float32)
            acc += jnp.dot(tok[1, zz, cc, span], wts[xx, pl.ds(feats, feats)], preferred_element_type=jnp.float32)
            top = jnp.max(acc.reshape(per // 2, tokens_per, cols), axis=1)
            top = jnp.log1p(jnp.maximum(top, 0.0))
            both = jnp.concatenate([top, top], axis=0)
            place = lax.broadcasted_iota(jnp.int32, both.shape, 0) // (per // 2)
            first = pl.multiple_of((zz * CS + cc) * per, per)
            old = jnp.where(h == 0, 0.0, pool[xx, pl.ds(first, per), :])
            pool[xx, pl.ds(first, per), :] = jnp.where(place == h, both, old)
            return carry

        lax.fori_loop(0, CS * XS, part, 0)

    hops = (ZS - 1) * CHUNKS

    def event(e, carry):
        @pl.when(e < hops)
        def _():
            pass_tokens(1 + e // CHUNKS, lax.rem(e, CHUNKS))

        @pl.when(e == 0)
        def _():
            pass_head(z, 1 - c)

        for d in range(1, ZS):
            @pl.when(e == d * CHUNKS // ZS)
            def _():
                near_head(d)

        @pl.when(e == CHUNKS)
        def _():
            from_y(z)

        @pl.when(e == lead)
        def _():
            for i in range(ZS * CS):
                relay(i // CS, i % CS).wait_recv()

        j = (e - lead) // (CHUNKS // 4)
        low = z < ZS // 2
        near = jnp.where(z == 0, 1, z - 1)
        far = jnp.where(z == ZS - 1, -1, z + 1)
        zz = jnp.where(j == 0, z, jnp.where(j == 1, near, jnp.where(j == 2, far, jnp.where(
            j == 3, jnp.where(low, z + 2, z - 2), jnp.where(low, z + 3, z - 3)))))
        there = (j >= 0) & (j < 6) & (lax.rem(e - lead, CHUNKS // 4) == 0) & (zz >= 0) & (zz < ZS)
        there = there & ((j != 2) | (z > 0))
        begin = jnp.where(j == 5, 1, 0)
        end = jnp.where(j == 4, 1, 2)

        @pl.when(there)
        def _():
            def halves(h, inner):
                @pl.when(j > 0)
                def _():
                    for k in range(CHUNKS // 2):
                        at_k = h * (CHUNKS // 2) + k
                        src = piece(1 - y, zz, c, at_k)
                        across_y(zz, at_k, src).wait_recv()
                        across_c(1 - y, zz, at_k, src).start()

                arrived(zz, h)
                multiply(zz, h)
                return inner

            lax.fori_loop(begin, end, halves, 0)

        return carry

    lead = hops - 5 * CHUNKS // 4
    lax.fori_loop(0, hops + CHUNKS // 4, event, 0)

    give[...] = pool[1 - x].astype(jnp.bfloat16)
    last = remote(give, take, s_f, r_f, x_dev)
    last.start()

    def sent(zz, carry):
        for k in range(CHUNKS):
            @pl.when((zz <= z) & (z < ZS - 1))
            def _():
                up(zz, k, own_piece(k)).wait_send()

            @pl.when((zz >= z) & (z > 0))
            def _():
                down(zz, k, own_piece(k)).wait_send()

            across_y(zz, k, own_piece(k)).wait_send()
            for f in range(2):
                across_c(f, zz, k, own_piece(k)).wait_send()
        for cc in range(CS):
            relay(zz, cc).wait_send()
        return carry

    lax.fori_loop(0, ZS, sent, 0)

    def head_sent(zz, cc):
        for xx in range(XS):
            head_to(zz, cc, xx).wait_send()

    others(head_sent)
    last.wait()

    mine = pool[x].astype(jnp.bfloat16).astype(jnp.float32)
    theirs = take[...].astype(jnp.float32)
    even = jnp.where(x == 0, mine, theirs)
    odd = jnp.where(x == 0, theirs, mine)
    span = CS * per
    parts = []
    for zz in range(ZS):
        parts += [even[zz * span:(zz + 1) * span], odd[zz * span:(zz + 1) * span]]
    full = jnp.concatenate(parts, axis=0)
    peak = jnp.max(full, axis=0, keepdims=True)
    out[...] = jnp.transpose(full / (1.0 + peak)).astype(jnp.bfloat16)


def masked(hidden, lengths):
    passages = lengths.shape[0]
    tokens_per = hidden.shape[0] // passages
    allowed = jnp.arange(tokens_per, dtype=jnp.int32)[None, :] < lengths[:, None]
    return jnp.where(allowed.reshape(-1)[:, None], hidden, jnp.bfloat16(0.0))


def fused(hidden, head_weight, lengths):
    passages = lengths.shape[0]
    tokens = hidden.shape[0]
    feats = hidden.shape[1]
    feat_rows = head_weight.shape[0]
    cols = head_weight.shape[1] // (ZS * XS * CS)
    rows = ZS * CS * passages
    dma = pltpu.SemaphoreType.DMA
    return pl.pallas_call(
        functools.partial(kernel, tokens // passages),
        out_shape=jax.ShapeDtypeStruct((cols, XS * rows), jnp.bfloat16),
        in_specs=[pl.BlockSpec(memory_space=pltpu.SMEM)] + [pl.BlockSpec(memory_space=pl.ANY)] * 2,
        out_specs=pl.BlockSpec(memory_space=pltpu.VMEM),
        scratch_shapes=[
            pltpu.VMEM((2, ZS, CS, tokens, feats), jnp.bfloat16),
            pltpu.VMEM((XS, 2 * feats, cols), jnp.bfloat16),
            pltpu.VMEM((XS, rows, cols), jnp.float32),
            pltpu.VMEM((rows, cols), jnp.bfloat16),
            pltpu.VMEM((rows, cols), jnp.bfloat16),
            dma((ZS, CHUNKS)), dma((ZS, CHUNKS)), dma((ZS, CHUNKS)),
            dma((ZS, CHUNKS)), dma((ZS, CHUNKS)),
            dma((2, ZS, CHUNKS)), dma((2, ZS, CHUNKS)),
            dma((ZS * CS, XS)), dma((ZS * CS, XS)),
            dma((ZS * CS,)), dma((ZS * CS,)),
            dma, dma, dma((XS,)), dma((CHUNKS,)),
        ],
        compiler_params=pltpu.CompilerParams(
            collective_id=0, has_side_effects=True, vmem_limit_bytes=HIGHEST_VMEM
        ),
        cost_estimate=pl.CostEstimate(
            flops=2 * ZS * CS * tokens * 2 * feats * XS * cols,
            bytes_accessed=2 * (tokens * feats + feat_rows * head_weight.shape[1]),
            transcendentals=0,
        ),
    )(lengths, hidden, head_weight)


def general(hidden, head_weight, lengths):
    terms = lax.axis_size("term")
    owners = lax.axis_size("pass")
    passages = lengths.shape[0]
    tokens_per = hidden.shape[0] // passages
    range_cols = head_weight.shape[1] // owners
    own = lax.all_to_all(masked(hidden, lengths), "term", split_axis=0, concat_axis=1, tiled=True)
    tokens = lax.all_gather(own, "pass", axis=0, tiled=True)
    rows = lax.all_to_all(head_weight, "pass", split_axis=1, concat_axis=0, tiled=True)
    weights = lax.all_gather(rows, "term", axis=1, tiled=True)
    share = passages // terms
    logits = jnp.dot(tokens, weights, preferred_element_type=jnp.float32)
    logits = logits.reshape(owners * share, tokens_per, terms * range_cols)
    top = jnp.maximum(jnp.max(logits, axis=1), jnp.float32(0.0))
    pooled = jnp.log1p(top).astype(jnp.bfloat16)
    got = lax.all_to_all(
        pooled.reshape(owners * share, terms, range_cols), "term", split_axis=1, concat_axis=1, tiled=True
    )
    full = got.reshape(owners, share, terms, range_cols).transpose(0, 2, 1, 3)
    full = full.reshape(owners * passages, range_cols).astype(jnp.float32)
    peak = jnp.max(full, axis=0)
    return jnp.transpose((full / (1.0 + peak)[None, :]).astype(jnp.bfloat16))


def solution(mesh):
    small = mesh.shape["term"] == 2 and mesh.shape["pass"] == ZS * XS * CS
    return jax.shard_map(
        fused if small else general,
        mesh=mesh,
        in_specs=(P("pass", "term"), P("pass", "term"), P("pass")),
        out_specs=P(("term", "pass"), None),
        check_vma=False,
    )
```

```python
import functools

import jax
import jax.numpy as jnp
from jax import lax
from jax.experimental import pallas as pl
from jax.experimental.pallas import tpu as pltpu
from jax.sharding import PartitionSpec as P

MESH = pl.DeviceIdType.MESH
ZS, XS, CS = 4, 2, 2
CHUNKS = 4
HIGHEST_VMEM = 58 * 1024 * 1024


def kernel(
    tokens_per, lens, hid, head, out,
    tok, wts, pool, give, take,
    s_up, s_dn, r_z, s_y, r_y, s_c, r_c, s_h, r_h, s_x, r_x, s_f, r_f, s_l, s_t,
):
    y = lax.axis_index("term")
    me = lax.axis_index("pass")
    z, x, c = me // (XS * CS), (me // CS) % XS, me % CS
    block, feats = hid.shape
    feat_rows = head.shape[0]
    cols = wts.shape[2]
    rows = block // CHUNKS
    per = block // tokens_per

    def at(zz, xx, cc):
        return (zz * XS + xx) * CS + cc

    y_dev = (1 - y, me)
    x_dev = (y, at(z, 1 - x, c))
    c_dev = (y, at(z, x, 1 - c))
    up_dev = (y, at(jnp.minimum(z + 1, ZS - 1), x, c))
    dn_dev = (y, at(jnp.maximum(z - 1, 0), x, c))

    def others(do):
        for i in range(1, ZS):
            zz = lax.rem(z + i, ZS)
            for cc in range(CS):
                do(zz, cc)
        do(z, 1 - c)

    loads = [
        pltpu.make_async_copy(
            hid.at[pl.ds(k * rows, rows)], tok.at[y, z, c, pl.ds(k * rows, rows)], s_t.at[k]
        )
        for k in range(CHUNKS)
    ]
    for load in loads:
        load.start()

    barrier = pltpu.get_barrier_semaphore()

    def hello(dev):
        pl.semaphore_signal(barrier, inc=1, device_id=dev, device_id_type=MESH)

    others(lambda zz, cc: hello((y, at(zz, x, cc))))
    hello(x_dev)
    hello(y_dev)
    pl.semaphore_wait(barrier, ZS * CS + 1)

    def remote(src, dst, send, recv, dev):
        return pltpu.make_async_remote_copy(
            src_ref=src, dst_ref=dst, send_sem=send, recv_sem=recv,
            device_id=dev, device_id_type=MESH,
        )

    def piece(f, zz, cc, k):
        return tok.at[f, zz, cc, pl.ds(k * rows, rows)]

    def own_piece(k):
        return piece(y, z, c, k)

    def up(zz, k, src):
        return remote(src, piece(y, zz, c, k), s_up.at[zz, k], r_z.at[zz, k], up_dev)

    def down(zz, k, src):
        return remote(src, piece(y, zz, c, k), s_dn.at[zz, k], r_z.at[zz, k], dn_dev)

    def across_y(zz, k, src):
        return remote(src, piece(y, zz, c, k), s_y.at[zz, k], r_y.at[zz, k], y_dev)

    def across_c(f, zz, k, src):
        return remote(src, piece(f, zz, c, k), s_c.at[f, zz, k], r_c.at[f, zz, k], c_dev)

    def strip(zz, cc, xx):
        first = at(zz, xx, cc) * cols
        return head.at[:, pl.ds(pl.multiple_of(first, cols), cols)]

    def wts_of(p, xx):
        return wts.at[xx, pl.ds(pl.multiple_of(p * feat_rows, feat_rows), feat_rows)]

    def both_of(p):
        return wts.at[:, pl.ds(pl.multiple_of(p * feat_rows, feat_rows), feat_rows)]

    def head_to(zz, cc, xx):
        return remote(
            strip(zz, cc, xx), wts_of(me, xx),
            s_h.at[zz * CS + cc, xx], r_h.at[z * CS + c, xx], (y, at(zz, x, cc)),
        )

    def head_from(zz, cc, xx):
        ref = wts_of(at(zz, x, cc), xx)
        return remote(ref, ref, s_h.at[zz * CS + cc, xx], r_h.at[zz * CS + cc, xx], x_dev)

    def relay(zz, cc):
        ref = both_of(at(zz, x, cc))
        return remote(ref, ref, s_x.at[zz * CS + cc], r_x.at[zz * CS + cc], x_dev)

    def send_head(zz, cc):
        for xx in range(XS):
            head_to(zz, cc, xx).start()

    def pass_head(zz, cc):
        for xx in range(XS):
            head_from(zz, cc, xx).wait_recv()
        relay(zz, cc).start()

    def sides(d, do):
        def side(s, inner):
            zz = z + (1 - 2 * s) * d

            @pl.when((zz >= 0) & (zz < ZS))
            def _():
                do(zz)

            return inner

        lax.fori_loop(0, 2, side, 0)

    def pass_tokens(d, k):
        below, above = z - d, z + d

        @pl.when(below >= 0)
        def _():
            src = piece(y, below, c, k)
            up(below, k, src).wait_recv()

            @pl.when(z < ZS - 1)
            def _():
                up(below, k, src).start()

            across_y(below, k, src).start()
            across_c(y, below, k, src).start()

        @pl.when(above < ZS)
        def _():
            src = piece(y, above, c, k)
            down(above, k, src).wait_recv()

            @pl.when(z > 0)
            def _():
                down(above, k, src).start()

            across_y(above, k, src).start()
            across_c(y, above, k, src).start()

    def from_y(zz):
        def one(k, carry):
            src = piece(1 - y, zz, c, k)
            across_y(zz, k, src).wait_recv()
            across_c(1 - y, zz, k, src).start()
            return carry

        lax.fori_loop(0, CHUNKS, one, 0)

    def near_head(d):
        def both(zz):
            for cc in range(CS):
                pass_head(zz, cc)

        sides(d, both)

    local = [pltpu.make_async_copy(strip(z, c, xx), wts_of(me, xx), s_l.at[xx]) for xx in range(XS)]
    send_head(z, 1 - c)
    for copy in local:
        copy.start()

    slots = lax.broadcasted_iota(jnp.int32, (tokens_per, feats), 0)
    for k in range(CHUNKS):
        loads[k].wait()
        for i in range(k * rows // tokens_per, (k + 1) * rows // tokens_per):
            own = (y, z, c, pl.ds(i * tokens_per, tokens_per))
            kept = jnp.where(slots < lens[i], tok[own].astype(jnp.float32), 0.0)
            tok[own] = kept.astype(jnp.bfloat16)

    def send_own(k, carry):
        @pl.when(z < ZS - 1)
        def _():
            up(z, k, own_piece(k)).start()

        @pl.when(z > 0)
        def _():
            down(z, k, own_piece(k)).start()

        across_y(z, k, own_piece(k)).start()
        across_c(y, z, k, own_piece(k)).start()

        for i in range(1, ZS):
            @pl.when(k == i * CHUNKS // ZS - 1)
            def _():
                def strips(zz):
                    for cc in range(CS):
                        send_head(zz, cc)

                sides(i, strips)

        return carry

    lax.fori_loop(0, CHUNKS, send_own, 0)
    for copy in local:
        copy.wait()
    relay(z, c).start()

    def arrived(zz):
        for f in range(2):
            for k in range(CHUNKS):
                across_c(f, zz, k, piece(f, zz, 1 - c, k)).wait_recv()

    def multiply(zz):
        def half(xx, carry):
            first, second = (tok[f, zz].reshape(CS * block, feats) for f in range(2))
            acc = jnp.dot(first, wts[xx, pl.ds(0, feats)], preferred_element_type=jnp.float32)
            acc += jnp.dot(second, wts[xx, pl.ds(feats, feats)], preferred_element_type=jnp.float32)
            top = jnp.max(acc.reshape(CS * per, tokens_per, cols), axis=1)
            place = pl.ds(pl.multiple_of(zz * CS * per, CS * per), CS * per)
            pool[xx, place, :] = jnp.log1p(jnp.maximum(top, 0.0))
            return carry

        lax.fori_loop(0, XS, half, 0)

    hops = (ZS - 1) * CHUNKS

    def event(e, carry):
        @pl.when(e < hops)
        def _():
            pass_tokens(1 + e // CHUNKS, lax.rem(e, CHUNKS))

        @pl.when(e == 0)
        def _():
            pass_head(z, 1 - c)

        for d in range(1, ZS):
            @pl.when(e == d * CHUNKS // ZS)
            def _():
                near_head(d)

        @pl.when(e == CHUNKS)
        def _():
            from_y(z)

        @pl.when(e == lead)
        def _():
            for i in range(ZS * CS):
                relay(i // CS, i % CS).wait_recv()

        j = e - lead
        low = z < ZS // 2
        near = jnp.where(z == 0, 1, z - 1)
        far = jnp.where((z == 0) | (z == ZS - 1), -1, z + 1)
        zz = jnp.where(j == 0, z, jnp.where(j == 1, near, jnp.where(j == 2, far, jnp.where(
            j == 3, jnp.where(low, z + 2, z - 2), jnp.where(low, z + 3, z - 3)))))

        @pl.when((j >= 0) & (j != 4) & (zz >= 0) & (zz < ZS))
        def _():
            @pl.when(j > 0)
            def _():
                from_y(zz)

            arrived(zz)
            multiply(zz)

        return carry

    lead = hops - 5 * CHUNKS // 4
    lax.fori_loop(0, hops + CHUNKS // 4, event, 0)

    give[...] = pool[1 - x].astype(jnp.bfloat16)
    last = remote(give, take, s_f, r_f, x_dev)
    last.start()

    def sent(zz, carry):
        for k in range(CHUNKS):
            @pl.when((zz <= z) & (z < ZS - 1))
            def _():
                up(zz, k, own_piece(k)).wait_send()

            @pl.when((zz >= z) & (z > 0))
            def _():
                down(zz, k, own_piece(k)).wait_send()

            across_y(zz, k, own_piece(k)).wait_send()
            for f in range(2):
                across_c(f, zz, k, own_piece(k)).wait_send()
        for cc in range(CS):
            relay(zz, cc).wait_send()
        return carry

    lax.fori_loop(0, ZS, sent, 0)

    def head_sent(zz, cc):
        for xx in range(XS):
            head_to(zz, cc, xx).wait_send()

    others(head_sent)
    last.wait()

    mine = pool[x].astype(jnp.bfloat16).astype(jnp.float32)
    theirs = take[...].astype(jnp.float32)
    even = jnp.where(x == 0, mine, theirs)
    odd = jnp.where(x == 0, theirs, mine)
    span = CS * per
    parts = []
    for zz in range(ZS):
        parts += [even[zz * span:(zz + 1) * span], odd[zz * span:(zz + 1) * span]]
    full = jnp.concatenate(parts, axis=0)
    peak = jnp.max(full, axis=0, keepdims=True)
    out[...] = jnp.transpose(full / (1.0 + peak)).astype(jnp.bfloat16)


def masked(hidden, lengths):
    passages = lengths.shape[0]
    tokens_per = hidden.shape[0] // passages
    allowed = jnp.arange(tokens_per, dtype=jnp.int32)[None, :] < lengths[:, None]
    return jnp.where(allowed.reshape(-1)[:, None], hidden, jnp.bfloat16(0.0))


def fused(hidden, head_weight, lengths):
    passages = lengths.shape[0]
    tokens = hidden.shape[0]
    feats = hidden.shape[1]
    feat_rows = head_weight.shape[0]
    cols = head_weight.shape[1] // (ZS * XS * CS)
    rows = ZS * CS * passages
    dma = pltpu.SemaphoreType.DMA
    return pl.pallas_call(
        functools.partial(kernel, tokens // passages),
        out_shape=jax.ShapeDtypeStruct((cols, XS * rows), jnp.bfloat16),
        in_specs=[pl.BlockSpec(memory_space=pltpu.SMEM)] + [pl.BlockSpec(memory_space=pl.ANY)] * 2,
        out_specs=pl.BlockSpec(memory_space=pltpu.VMEM),
        scratch_shapes=[
            pltpu.VMEM((2, ZS, CS, tokens, feats), jnp.bfloat16),
            pltpu.VMEM((XS, 2 * feats, cols), jnp.bfloat16),
            pltpu.VMEM((XS, rows, cols), jnp.float32),
            pltpu.VMEM((rows, cols), jnp.bfloat16),
            pltpu.VMEM((rows, cols), jnp.bfloat16),
            dma((ZS, CHUNKS)), dma((ZS, CHUNKS)), dma((ZS, CHUNKS)),
            dma((ZS, CHUNKS)), dma((ZS, CHUNKS)),
            dma((2, ZS, CHUNKS)), dma((2, ZS, CHUNKS)),
            dma((ZS * CS, XS)), dma((ZS * CS, XS)),
            dma((ZS * CS,)), dma((ZS * CS,)),
            dma, dma, dma((XS,)), dma((CHUNKS,)),
        ],
        compiler_params=pltpu.CompilerParams(
            collective_id=0, has_side_effects=True, vmem_limit_bytes=HIGHEST_VMEM
        ),
        cost_estimate=pl.CostEstimate(
            flops=2 * ZS * CS * tokens * 2 * feats * XS * cols,
            bytes_accessed=2 * (tokens * feats + feat_rows * head_weight.shape[1]),
            transcendentals=0,
        ),
    )(lengths, hidden, head_weight)


def general(hidden, head_weight, lengths):
    terms = lax.axis_size("term")
    owners = lax.axis_size("pass")
    passages = lengths.shape[0]
    tokens_per = hidden.shape[0] // passages
    range_cols = head_weight.shape[1] // owners
    own = lax.all_to_all(masked(hidden, lengths), "term", split_axis=0, concat_axis=1, tiled=True)
    tokens = lax.all_gather(own, "pass", axis=0, tiled=True)
    rows = lax.all_to_all(head_weight, "pass", split_axis=1, concat_axis=0, tiled=True)
    weights = lax.all_gather(rows, "term", axis=1, tiled=True)
    share = passages // terms
    logits = jnp.dot(tokens, weights, preferred_element_type=jnp.float32)
    logits = logits.reshape(owners * share, tokens_per, terms * range_cols)
    top = jnp.maximum(jnp.max(logits, axis=1), jnp.float32(0.0))
    pooled = jnp.log1p(top).astype(jnp.bfloat16)
    got = lax.all_to_all(
        pooled.reshape(owners * share, terms, range_cols), "term", split_axis=1, concat_axis=1, tiled=True
    )
    full = got.reshape(owners, share, terms, range_cols).transpose(0, 2, 1, 3)
    full = full.reshape(owners * passages, range_cols).astype(jnp.float32)
    peak = jnp.max(full, axis=0)
    return jnp.transpose((full / (1.0 + peak)[None, :]).astype(jnp.bfloat16))


def solution(mesh):
    small = mesh.shape["term"] == 2 and mesh.shape["pass"] == ZS * XS * CS
    return jax.shard_map(
        fused if small else general,
        mesh=mesh,
        in_specs=(P("pass", "term"), P("pass", "term"), P("pass")),
        out_specs=P(("term", "pass"), None),
        check_vma=False,
    )
```

```python
import functools

import jax
import jax.numpy as jnp
from jax import lax
from jax.experimental import pallas as pl
from jax.experimental.pallas import tpu as pltpu
from jax.sharding import PartitionSpec as P

MESH = pl.DeviceIdType.MESH
ZS, XS, CS = 4, 2, 2
CHUNKS = 4
HIGHEST_VMEM = 58 * 1024 * 1024


def kernel(
    tokens_per, lens, hid, head, out,
    tok, wts, pool, give, take,
    s_up, s_dn, r_z, s_y, r_y, s_c, r_c, s_h, r_h, s_x, r_x, s_f, r_f, s_l, s_t,
):
    y = lax.axis_index("term")
    me = lax.axis_index("pass")
    z, x, c = me // (XS * CS), (me // CS) % XS, me % CS
    block, feats = hid.shape
    feat_rows = head.shape[0]
    cols = wts.shape[2]
    rows = block // CHUNKS
    per = block // tokens_per

    def at(zz, xx, cc):
        return (zz * XS + xx) * CS + cc

    y_dev = (1 - y, me)
    x_dev = (y, at(z, 1 - x, c))
    c_dev = (y, at(z, x, 1 - c))
    up_dev = (y, at(jnp.minimum(z + 1, ZS - 1), x, c))
    dn_dev = (y, at(jnp.maximum(z - 1, 0), x, c))

    def others(do):
        for i in range(1, ZS):
            zz = lax.rem(z + i, ZS)
            for cc in range(CS):
                do(zz, cc)
        do(z, 1 - c)

    loads = [
        pltpu.make_async_copy(
            hid.at[pl.ds(k * rows, rows)], tok.at[y, z, c, pl.ds(k * rows, rows)], s_t.at[k]
        )
        for k in range(CHUNKS)
    ]
    for load in loads:
        load.start()

    barrier = pltpu.get_barrier_semaphore()

    def hello(dev):
        pl.semaphore_signal(barrier, inc=1, device_id=dev, device_id_type=MESH)

    others(lambda zz, cc: hello((y, at(zz, x, cc))))
    hello(x_dev)
    hello(y_dev)
    pl.semaphore_wait(barrier, ZS * CS + 1)

    def remote(src, dst, send, recv, dev):
        return pltpu.make_async_remote_copy(
            src_ref=src, dst_ref=dst, send_sem=send, recv_sem=recv,
            device_id=dev, device_id_type=MESH,
        )

    def piece(f, zz, cc, k):
        return tok.at[f, zz, cc, pl.ds(k * rows, rows)]

    def own_piece(k):
        return piece(y, z, c, k)

    def up(zz, k, src):
        return remote(src, piece(y, zz, c, k), s_up.at[zz, k], r_z.at[zz, k], up_dev)

    def down(zz, k, src):
        return remote(src, piece(y, zz, c, k), s_dn.at[zz, k], r_z.at[zz, k], dn_dev)

    def across_y(zz, k, src):
        return remote(src, piece(y, zz, c, k), s_y.at[zz, k], r_y.at[zz, k], y_dev)

    def across_c(f, zz, k, src):
        return remote(src, piece(f, zz, c, k), s_c.at[f, zz, k], r_c.at[f, zz, k], c_dev)

    def strip(zz, cc, xx):
        first = at(zz, xx, cc) * cols
        return head.at[:, pl.ds(pl.multiple_of(first, cols), cols)]

    def wts_of(p, xx):
        return wts.at[xx, pl.ds(pl.multiple_of(p * feat_rows, feat_rows), feat_rows)]

    def both_of(p):
        return wts.at[:, pl.ds(pl.multiple_of(p * feat_rows, feat_rows), feat_rows)]

    def head_to(zz, cc, xx):
        return remote(
            strip(zz, cc, xx), wts_of(me, xx),
            s_h.at[zz * CS + cc, xx], r_h.at[z * CS + c, xx], (y, at(zz, x, cc)),
        )

    def head_from(zz, cc, xx):
        ref = wts_of(at(zz, x, cc), xx)
        return remote(ref, ref, s_h.at[zz * CS + cc, xx], r_h.at[zz * CS + cc, xx], x_dev)

    def relay(zz, cc):
        ref = both_of(at(zz, x, cc))
        return remote(ref, ref, s_x.at[zz * CS + cc], r_x.at[zz * CS + cc], x_dev)

    def send_head(zz, cc):
        for xx in range(XS):
            head_to(zz, cc, xx).start()

    def pass_head(zz, cc):
        for xx in range(XS):
            head_from(zz, cc, xx).wait_recv()
        relay(zz, cc).start()

    def sides(d, do):
        def side(s, inner):
            zz = z + (1 - 2 * s) * d

            @pl.when((zz >= 0) & (zz < ZS))
            def _():
                do(zz)

            return inner

        lax.fori_loop(0, 2, side, 0)

    def pass_tokens(d, k):
        below, above = z - d, z + d

        @pl.when(below >= 0)
        def _():
            src = piece(y, below, c, k)
            up(below, k, src).wait_recv()

            @pl.when(z < ZS - 1)
            def _():
                up(below, k, src).start()

            across_y(below, k, src).start()
            across_c(y, below, k, src).start()

        @pl.when(above < ZS)
        def _():
            src = piece(y, above, c, k)
            down(above, k, src).wait_recv()

            @pl.when(z > 0)
            def _():
                down(above, k, src).start()

            across_y(above, k, src).start()
            across_c(y, above, k, src).start()

    def from_y(zz):
        def one(k, carry):
            src = piece(1 - y, zz, c, k)
            across_y(zz, k, src).wait_recv()
            across_c(1 - y, zz, k, src).start()
            return carry

        lax.fori_loop(0, CHUNKS, one, 0)

    def near_head(d):
        def both(zz):
            for cc in range(CS):
                pass_head(zz, cc)

        sides(d, both)

    local = [pltpu.make_async_copy(strip(z, c, xx), wts_of(me, xx), s_l.at[xx]) for xx in range(XS)]
    send_head(z, 1 - c)
    for copy in local:
        copy.start()

    slots = lax.broadcasted_iota(jnp.int32, (tokens_per, feats), 0)
    for k in range(CHUNKS):
        loads[k].wait()
        for i in range(k * rows // tokens_per, (k + 1) * rows // tokens_per):
            own = (y, z, c, pl.ds(i * tokens_per, tokens_per))
            kept = jnp.where(slots < lens[i], tok[own].astype(jnp.float32), 0.0)
            tok[own] = kept.astype(jnp.bfloat16)

    def send_own(k, carry):
        @pl.when(z < ZS - 1)
        def _():
            up(z, k, own_piece(k)).start()

        @pl.when(z > 0)
        def _():
            down(z, k, own_piece(k)).start()

        across_y(z, k, own_piece(k)).start()
        across_c(y, z, k, own_piece(k)).start()

        for i in range(1, ZS):
            @pl.when(k == i * CHUNKS // ZS - 1)
            def _():
                def strips(zz):
                    for cc in range(CS):
                        send_head(zz, cc)

                sides(i, strips)

        return carry

    lax.fori_loop(0, CHUNKS, send_own, 0)
    for copy in local:
        copy.wait()
    relay(z, c).start()

    def arrived(zz):
        for f in range(2):
            for k in range(CHUNKS):
                across_c(f, zz, k, piece(f, zz, 1 - c, k)).wait_recv()

    def multiply(zz):
        def half(xx, carry):
            first, second = (tok[f, zz].reshape(CS * block, feats) for f in range(2))
            acc = jnp.dot(first, wts[xx, pl.ds(0, feats)], preferred_element_type=jnp.float32)
            acc += jnp.dot(second, wts[xx, pl.ds(feats, feats)], preferred_element_type=jnp.float32)
            top = jnp.max(acc.reshape(CS * per, tokens_per, cols), axis=1)
            place = pl.ds(pl.multiple_of(zz * CS * per, CS * per), CS * per)
            pool[xx, place, :] = jnp.log1p(jnp.maximum(top, 0.0))
            return carry

        lax.fori_loop(0, XS, half, 0)

    hops = (ZS - 1) * CHUNKS

    def event(e, carry):
        @pl.when(e < hops)
        def _():
            pass_tokens(1 + e // CHUNKS, lax.rem(e, CHUNKS))

        @pl.when(e == 0)
        def _():
            pass_head(z, 1 - c)

        for d in range(1, ZS):
            @pl.when(e == d * CHUNKS // ZS)
            def _():
                near_head(d)

        @pl.when(e == CHUNKS)
        def _():
            from_y(z)

        @pl.when(e == lead)
        def _():
            for i in range(ZS * CS):
                relay(i // CS, i % CS).wait_recv()

        j = e - lead
        low = z < ZS // 2
        near = jnp.where(z == 0, 1, z - 1)
        far = jnp.where((z == 0) | (z == ZS - 1), -1, z + 1)
        zz = jnp.where(j == 0, z, jnp.where(j == 1, near, jnp.where(j == 2, far, jnp.where(
            j == 4, jnp.where(low, z + 2, z - 2), jnp.where(low, z + 3, z - 3)))))

        @pl.when((j >= 0) & (j != 3) & (zz >= 0) & (zz < ZS))
        def _():
            @pl.when(j > 0)
            def _():
                from_y(zz)

            arrived(zz)
            multiply(zz)

        return carry

    lead = hops - 5 * CHUNKS // 4
    lax.fori_loop(0, hops + CHUNKS // 4, event, 0)

    give[...] = pool[1 - x].astype(jnp.bfloat16)
    last = remote(give, take, s_f, r_f, x_dev)
    last.start()

    def sent(zz, carry):
        for k in range(CHUNKS):
            @pl.when((zz <= z) & (z < ZS - 1))
            def _():
                up(zz, k, own_piece(k)).wait_send()

            @pl.when((zz >= z) & (z > 0))
            def _():
                down(zz, k, own_piece(k)).wait_send()

            across_y(zz, k, own_piece(k)).wait_send()
            for f in range(2):
                across_c(f, zz, k, own_piece(k)).wait_send()
        for cc in range(CS):
            relay(zz, cc).wait_send()
        return carry

    lax.fori_loop(0, ZS, sent, 0)

    def head_sent(zz, cc):
        for xx in range(XS):
            head_to(zz, cc, xx).wait_send()

    others(head_sent)
    last.wait()

    mine = pool[x].astype(jnp.bfloat16).astype(jnp.float32)
    theirs = take[...].astype(jnp.float32)
    even = jnp.where(x == 0, mine, theirs)
    odd = jnp.where(x == 0, theirs, mine)
    span = CS * per
    parts = []
    for zz in range(ZS):
        parts += [even[zz * span:(zz + 1) * span], odd[zz * span:(zz + 1) * span]]
    full = jnp.concatenate(parts, axis=0)
    peak = jnp.max(full, axis=0, keepdims=True)
    out[...] = jnp.transpose(full / (1.0 + peak)).astype(jnp.bfloat16)


def masked(hidden, lengths):
    passages = lengths.shape[0]
    tokens_per = hidden.shape[0] // passages
    allowed = jnp.arange(tokens_per, dtype=jnp.int32)[None, :] < lengths[:, None]
    return jnp.where(allowed.reshape(-1)[:, None], hidden, jnp.bfloat16(0.0))


def fused(hidden, head_weight, lengths):
    passages = lengths.shape[0]
    tokens = hidden.shape[0]
    feats = hidden.shape[1]
    feat_rows = head_weight.shape[0]
    cols = head_weight.shape[1] // (ZS * XS * CS)
    rows = ZS * CS * passages
    dma = pltpu.SemaphoreType.DMA
    return pl.pallas_call(
        functools.partial(kernel, tokens // passages),
        out_shape=jax.ShapeDtypeStruct((cols, XS * rows), jnp.bfloat16),
        in_specs=[pl.BlockSpec(memory_space=pltpu.SMEM)] + [pl.BlockSpec(memory_space=pl.ANY)] * 2,
        out_specs=pl.BlockSpec(memory_space=pltpu.VMEM),
        scratch_shapes=[
            pltpu.VMEM((2, ZS, CS, tokens, feats), jnp.bfloat16),
            pltpu.VMEM((XS, 2 * feats, cols), jnp.bfloat16),
            pltpu.VMEM((XS, rows, cols), jnp.float32),
            pltpu.VMEM((rows, cols), jnp.bfloat16),
            pltpu.VMEM((rows, cols), jnp.bfloat16),
            dma((ZS, CHUNKS)), dma((ZS, CHUNKS)), dma((ZS, CHUNKS)),
            dma((ZS, CHUNKS)), dma((ZS, CHUNKS)),
            dma((2, ZS, CHUNKS)), dma((2, ZS, CHUNKS)),
            dma((ZS * CS, XS)), dma((ZS * CS, XS)),
            dma((ZS * CS,)), dma((ZS * CS,)),
            dma, dma, dma((XS,)), dma((CHUNKS,)),
        ],
        compiler_params=pltpu.CompilerParams(
            collective_id=0, has_side_effects=True, vmem_limit_bytes=HIGHEST_VMEM
        ),
        cost_estimate=pl.CostEstimate(
            flops=2 * ZS * CS * tokens * 2 * feats * XS * cols,
            bytes_accessed=2 * (tokens * feats + feat_rows * head_weight.shape[1]),
            transcendentals=0,
        ),
    )(lengths, hidden, head_weight)


def general(hidden, head_weight, lengths):
    terms = lax.axis_size("term")
    owners = lax.axis_size("pass")
    passages = lengths.shape[0]
    tokens_per = hidden.shape[0] // passages
    range_cols = head_weight.shape[1] // owners
    own = lax.all_to_all(masked(hidden, lengths), "term", split_axis=0, concat_axis=1, tiled=True)
    tokens = lax.all_gather(own, "pass", axis=0, tiled=True)
    rows = lax.all_to_all(head_weight, "pass", split_axis=1, concat_axis=0, tiled=True)
    weights = lax.all_gather(rows, "term", axis=1, tiled=True)
    share = passages // terms
    logits = jnp.dot(tokens, weights, preferred_element_type=jnp.float32)
    logits = logits.reshape(owners * share, tokens_per, terms * range_cols)
    top = jnp.maximum(jnp.max(logits, axis=1), jnp.float32(0.0))
    pooled = jnp.log1p(top).astype(jnp.bfloat16)
    got = lax.all_to_all(
        pooled.reshape(owners * share, terms, range_cols), "term", split_axis=1, concat_axis=1, tiled=True
    )
    full = got.reshape(owners, share, terms, range_cols).transpose(0, 2, 1, 3)
    full = full.reshape(owners * passages, range_cols).astype(jnp.float32)
    peak = jnp.max(full, axis=0)
    return jnp.transpose((full / (1.0 + peak)[None, :]).astype(jnp.bfloat16))


def solution(mesh):
    small = mesh.shape["term"] == 2 and mesh.shape["pass"] == ZS * XS * CS
    return jax.shard_map(
        fused if small else general,
        mesh=mesh,
        in_specs=(P("pass", "term"), P("pass", "term"), P("pass")),
        out_specs=P(("term", "pass"), None),
        check_vma=False,
    )
```
